128 devices in a mesh: gx: 16 (over y, x), gy: 8 (over z, core).
Axes of the slice: x: 4, y: 4, z: 4, core: 2. Of those that a mesh axis runs over, the one named last changes fastest.
Arguments:
- u_init: bfloat16 [64, 128, 64, 128], P(None, 'gx', 'gy'), may hold values from -6 to 6
- rhs: bfloat16 [64, 128, 64, 128], P(None, 'gx', 'gy'), may hold values from -6 to 6
- kappa: float32 [128, 64, 128], P('gx', 'gy'), may hold values from 0.5 to 2
- block_diagonal: bfloat16 [64, 64], replicated, as said below
- face_coupling: bfloat16 [6, 64, 16], replicated, may hold values from -0.1796875 to 0.1796875
- smoother: bfloat16 [64, 64], replicated, as said below
- restriction: bfloat16 [8, 64], replicated, may hold values from -0.75 to 0.75
- coarse_inverse: float32 [8, 8, 262144], P(None, None, ('gx', 'gy')), may hold values from -12 to 12
- segment_id: int32 [128, 64, 128], P('gx', 'gy'), may hold values from 0 to 31, never falling along the last dimension, each value on 1 to 8 neighbouring positions
- owner_device: int32 [128, 64, 32], P('gx', 'gy'), may hold values from 0 to 127, as said below
- arrival_place: int32 [128, 128, 16], P(('gx', 'gy')), may hold values from 0 to 2047, as said below
Outputs:
- solution: float32 [64, 128, 64, 128], P(None, 'gx', 'gy')
The draws below stay inside these ranges and needn't reach their ends.
Inputs may be any that keep to these rules, and one draw needn't show every extreme that they name: `segment_id`: within each line of 128 elements along z the numbers never fall, every aggregate has 1 to 8 elements and one has exactly 8. `owner_device`: of the aggregates of one device, at most 16 are owned by any one other device, and exactly 16 by some other device; device d owns as many aggregates of device e as device e owns of device d. arrival_place[t, d, r] is the place at device t of the aggregate of device d with arrival number r; the places a device receives are distinct and are exactly the local numbers of its own aggregates that other devices own; entries with no aggregate are 0. `block_diagonal`: A sum of 4 times the identity and a dense part. `smoother`: A sum of 0.06 times the identity and a dense part.
All inputs are finite; a program needn't handle non-finite values.
Results may differ from the reference program's by a relative error of at most 0.005.
Values may be sent and summed in bfloat16 or wider, within the bound.
No kernel may reach another device: no remote copies, remote signals or barrier semaphores. Data moves between devices by JAX's collectives and lax.ppermute only.
A program may use at most 128 MiB of HBM per device.

```python
import math
import jax
import jax.numpy as jnp
import numpy as np
from jax import lax

NODES = 64
CMODES = 8
BX = 8
BY = 8
EZ = 128
NSWEEP = 3
AMAX = 8
ACAP = 16
EX = 128
EY = 64
ZAGG = 32
ASLOT = 2048
NCOARSE = 262144
N_GX = 16
N_GY = 8
DEVICES = 128


def share_counts(key):
    pair_draw = jax.random.randint(key, (DEVICES, DEVICES), ACAP // 2, ACAP + 1)
    row_ids = jnp.arange(DEVICES, dtype=jnp.int32)[:, None]
    col_ids = jnp.arange(DEVICES, dtype=jnp.int32)[None, :]
    counts = jnp.where(row_ids < col_ids, pair_draw, pair_draw.T)
    counts = jnp.where(col_ids == row_ids ^ 1, ACAP, counts)
    counts = jnp.where(row_ids == col_ids, 0, counts).astype(jnp.int32)
    sub_keys = jax.random.split(jax.random.fold_in(key, 11), DEVICES)
    orders = jax.vmap(lambda sub_key: jax.random.permutation(sub_key, ASLOT))(sub_keys).astype(jnp.int32)
    return (counts, orders)


def draw_owner_device(key, part):
    counts, orders = share_counts(key)
    bounds = jnp.cumsum(counts, axis=1)
    totals = bounds[:, -1]
    ranks = jnp.broadcast_to(jnp.arange(ASLOT, dtype=jnp.int32)[None, :], (DEVICES, ASLOT))
    targets = jax.vmap(lambda bound_row, rank_row: jnp.searchsorted(bound_row, rank_row, side='right'))(bounds, ranks)
    owner_of = jnp.where(ranks < totals[:, None], targets.astype(jnp.int32), jnp.arange(DEVICES, dtype=jnp.int32)[:, None])
    row_ids = jnp.broadcast_to(jnp.arange(DEVICES, dtype=jnp.int32)[:, None], (DEVICES, ASLOT))
    owner_flat = jnp.zeros((DEVICES, ASLOT), jnp.int32).at[row_ids, orders].set(owner_of)
    shaped = owner_flat.reshape(N_GX, N_GY, BX, BY, ZAGG)
    return jnp.transpose(shaped, (0, 2, 1, 3, 4)).reshape(EX, EY, ZAGG).astype(jnp.int32)


def draw_arrival_place(key, part):
    counts, orders = share_counts(key)
    starts = jnp.cumsum(counts, axis=0) - counts
    arrival = jnp.arange(ACAP, dtype=jnp.int32)[None, None, :]
    picks = jnp.minimum(starts.T[:, :, None] + arrival, ASLOT - 1)
    values = jax.vmap(lambda order_row, pick_rows: order_row[pick_rows])(orders, picks)
    valid = arrival < counts.T[:, :, None]
    return jnp.where(valid, values, 0).astype(jnp.int32)


def dense_part(key, scale):
    return jax.random.normal(key, (NODES, NODES), jnp.float32) * scale


def draw_block_diagonal(key, part):
    key = jax.random.fold_in(key, 7)
    return (4.0 * jnp.eye(NODES, dtype=jnp.float32) + dense_part(key, 0.1)).astype(jnp.bfloat16)


def draw_smoother(key, part):
    key = jax.random.fold_in(key, 9)
    return (0.06 * jnp.eye(NODES, dtype=jnp.float32) + dense_part(key, 0.0018)).astype(jnp.bfloat16)


def block_levels(key, extent, cuts, least, top_value):
    level, own = 1.0, jax.random.fold_in(key, 6)
    for dim, blocks in cuts:
        heights = jnp.exp(jax.random.uniform(jax.random.fold_in(own, dim), (blocks,), jnp.float32, least / len(cuts), top_value / len(cuts)))
        level = level * jnp.repeat(heights, extent[dim] // blocks).reshape([-1 if axis == dim else 1 for axis in range(len(extent))])
    return level


def length_profile(amount, total, reach, slope):
    portions = [(1 << 20) // math.isqrt(rank ** slope) + 1 for rank in range(2, amount + 1)]
    spare, holding = total - reach - (amount - 1), [1] * (amount - 1)
    while spare > 0:
        movable = [i for i in range(amount - 1) if holding[i] < reach]
        pool, remaining = sum([portions[i] for i in movable]), spare
        for i in movable:
            more = min(reach - holding[i], max(1, remaining * portions[i] // pool), spare)
            holding[i] = holding[i] + more
            spare = spare - more
    return np.array([reach] + holding)


def ragged_sizes(key, number_of, total, most, skew):
    if number_of == 2:
        one = jax.random.randint(key, (), max(1, total - most), min(most, total - 1) + 1)
        return jnp.stack([one, total - one])
    sizes = jnp.asarray(length_profile(number_of, total, most, skew), jnp.int32)
    couples = (number_of - 1) // 2
    giver, sink = sizes[1:1 + 2 * couples:2], sizes[2:2 + 2 * couples:2]
    room = jnp.minimum(giver - 1, most - sink)
    moved = jax.random.randint(jax.random.fold_in(key, 1), (couples,), 0, 1 << 20) % (room + 1)
    sizes = sizes.at[1:1 + 2 * couples:2].set(giver - moved).at[2:2 + 2 * couples:2].set(sink + moved)
    return sizes[jax.random.permutation(jax.random.fold_in(key, 2), number_of)]


def centred(key, extent, spread, limit, shards=(), kind=jnp.bfloat16):
    drawn = spread * jax.random.normal(key, extent, jnp.float32)
    if shards:
        drawn = drawn * block_levels(key, extent, shards, -0.22, 0.18)
    return jnp.clip(drawn, -limit, limit).astype(kind)


def setup_inputs(seed: int = 0) -> dict:
    arg_keys = jax.random.split(jax.random.key(seed), 12)
    return {
        "u_init": centred(arg_keys[0], (NODES, EX, EY, EZ), 1.0, 6.0, ((1, 16), (2, 8))),
        "rhs": centred(arg_keys[1], (NODES, EX, EY, EZ), 1.0, 6.0, ((1, 16), (2, 8))),
        "kappa": jnp.clip(jnp.exp(math.log(2.0) - 1.3862944 * jax.random.uniform(arg_keys[2], (EX, EY, EZ), jnp.float32) ** block_levels(arg_keys[2], (EX, EY, EZ), ((0, 16), (1, 8)), -0.2, 0.2)), 0.5, 2.0),
        "block_diagonal": draw_block_diagonal(jax.random.fold_in(arg_keys[11], 71), 0),
        "face_coupling": centred(arg_keys[4], (6, NODES, 16), 0.03, 0.1796875),
        "smoother": draw_smoother(jax.random.fold_in(arg_keys[11], 71), 0),
        "restriction": centred(arg_keys[6], (CMODES, NODES), NODES ** -0.5, 0.75),
        "coarse_inverse": centred(arg_keys[7], (CMODES, CMODES, NCOARSE), 2.0, 12.0, ((2, 128),), jnp.float32),
        "segment_id": jax.vmap(lambda own: jnp.searchsorted(jnp.cumsum(ragged_sizes(own, ZAGG, EZ, AMAX, 0)), jnp.arange(EZ), side="right"))(jax.random.split(arg_keys[8], EX * EY)).reshape((EX, EY, EZ)).astype(jnp.int32),
        "owner_device": draw_owner_device(jax.random.fold_in(arg_keys[11], 71), 0),
        "arrival_place": draw_arrival_place(jax.random.fold_in(arg_keys[11], 71), 0),
    }


def product(left, right):
    return jnp.einsum('pq,qyz->pyz', left.astype(jnp.float32), right.astype(jnp.float32))


def cube_face(block, axis, layer):
    cube = block.reshape((4, 4, 4) + block.shape[1:])
    sheet = lax.index_in_dim(cube, layer, axis, keepdims=False)
    return sheet.reshape((16,) + block.shape[1:])


def operate_slab(padded, row_index, diag_block, coupling):
    triple = lax.dynamic_slice_in_dim(padded, row_index, 3, 0)
    lower_slab = triple[0]
    middle = triple[1]
    upper_slab = triple[2]
    image = product(diag_block, middle)
    image = image + product(coupling[0], cube_face(upper_slab, 0, 0))
    image = image + product(coupling[1], cube_face(lower_slab, 0, 3))
    y_low = cube_face(middle, 1, 0)
    y_high = cube_face(middle, 1, 3)
    image = image + product(coupling[2], jnp.pad(y_low[:, 1:], ((0, 0), (0, 1), (0, 0))))
    image = image + product(coupling[3], jnp.pad(y_high[:, :-1], ((0, 0), (1, 0), (0, 0))))
    z_low = cube_face(middle, 2, 0)
    z_high = cube_face(middle, 2, 3)
    image = image + product(coupling[4], jnp.pad(z_low[:, :, 1:], ((0, 0), (0, 0), (0, 1))))
    image = image + product(coupling[5], jnp.pad(z_high[:, :, :-1], ((0, 0), (0, 0), (1, 0))))
    return image


def padded_weights(solution, kappa):
    weighted = (kappa[:, None] * solution).astype(jnp.bfloat16)
    return jnp.pad(weighted, ((1, 1), (0, 0), (0, 0), (0, 0)))


def smooth_once(solution, rhs_rows, kappa, diag_block, coupling, smoother):
    padded = padded_weights(solution, kappa)

    def one_row(row_index):
        image = operate_slab(padded, row_index, diag_block, coupling)
        residual = rhs_rows[row_index].astype(jnp.float32) - image
        update = product(smoother, residual.astype(jnp.bfloat16))
        return solution[row_index] + update / kappa[row_index][None]

    return lax.map(one_row, jnp.arange(EX, dtype=jnp.int32))


def residual_rows(solution, rhs_rows, kappa, diag_block, coupling):
    padded = padded_weights(solution, kappa)

    def one_row(row_index):
        image = operate_slab(padded, row_index, diag_block, coupling)
        return (rhs_rows[row_index].astype(jnp.float32) - image).astype(jnp.bfloat16)

    return lax.map(one_row, jnp.arange(EX, dtype=jnp.int32))


def slot_rank(owner):
    order = jnp.argsort(owner, stable=True).astype(jnp.int32)
    ordered = owner[order]
    first = jnp.searchsorted(ordered, owner, side="left").astype(jnp.int32)
    position = jnp.zeros(owner.shape, jnp.int32).at[order].set(jnp.arange(owner.shape[0], dtype=jnp.int32))
    return position - first


def by_device(array):
    tail = array.shape[3:]
    shaped = array.reshape((N_GX, BX, N_GY, BY, ZAGG) + tail)
    order = (0, 2, 1, 3, 4) + tuple(range(5, 5 + len(tail)))
    return jnp.transpose(shaped, order).reshape((DEVICES, ASLOT) + tail)


def from_device(array):
    tail = array.shape[2:]
    shaped = array.reshape((N_GX, N_GY, BX, BY, ZAGG) + tail)
    order = (0, 2, 1, 3, 4) + tuple(range(5, 5 + len(tail)))
    return jnp.transpose(shaped, order).reshape((EX * EY * ZAGG,) + tail)


def reference(u_init, rhs, kappa, block_diagonal, face_coupling, smoother, restriction, coarse_inverse, segment_id, owner_device, arrival_place):
    solution = jnp.transpose(u_init, (1, 0, 2, 3)).astype(jnp.float32)
    rhs_rows = jnp.transpose(rhs, (1, 0, 2, 3))
    for sweep_number in range(NSWEEP):
        solution = smooth_once(solution, rhs_rows, kappa, block_diagonal, face_coupling, smoother)
    fine_residual = residual_rows(solution, rhs_rows, kappa, block_diagonal, face_coupling)
    restricted = jnp.einsum('mq,xqyz->xyzm', restriction.astype(jnp.float32), fine_residual.astype(jnp.float32))
    line_ids = jnp.arange(EX * EY, dtype=jnp.int32).reshape(EX, EY, 1)
    aggregate = (line_ids * ZAGG + segment_id).reshape(-1)
    total_count = EX * EY * ZAGG
    coarse_rhs = jax.ops.segment_sum(restricted.reshape(-1, CMODES), aggregate, total_count)
    weight_sum = jax.ops.segment_sum(kappa.reshape(-1), aggregate, total_count)
    rhs_dev = by_device(coarse_rhs.reshape(EX, EY, ZAGG, CMODES))
    weight_dev = by_device(weight_sum.reshape(EX, EY, ZAGG))
    owner = by_device(owner_device)
    ranks = jax.vmap(slot_rank)(owner)
    source = jnp.arange(DEVICES, dtype=jnp.int32)[:, None]
    local_number = jnp.arange(ASLOT, dtype=jnp.int32)[None, :]
    far_place = arrival_place[owner, jnp.broadcast_to(source, owner.shape), jnp.minimum(ranks, ACAP - 1)]
    places = jnp.where(owner == source, local_number, far_place)
    column = (owner * ASLOT + places).reshape(-1)
    blocks = jnp.take(coarse_inverse, column, axis=2)
    coarse_fix = jnp.einsum('pqn,nq->np', blocks, rhs_dev.reshape(-1, CMODES), precision=lax.Precision.HIGHEST)
    coarse_fix = coarse_fix / weight_dev.reshape(-1)[:, None]
    coarse_fix = from_device(coarse_fix.reshape(DEVICES, ASLOT, CMODES))
    per_element = coarse_fix[aggregate].reshape(EX, EY, EZ, CMODES)
    solution = solution + jnp.einsum('mq,xyzm->xqyz', restriction.astype(jnp.float32), per_element, precision=lax.Precision.HIGHEST)
    for sweep_number in range(NSWEEP):
        solution = smooth_once(solution, rhs_rows, kappa, block_diagonal, face_coupling, smoother)
    return jnp.transpose(solution, (1, 0, 2, 3))
```

```python
import jax
import jax.numpy as jnp
from jax import lax
from jax.experimental import pallas as pl
from jax.experimental.pallas import tpu as pltpu
from jax.sharding import PartitionSpec as P


F32 = jnp.float32
BF16 = jnp.bfloat16
I32 = jnp.int32
LIMIT = 30 * 1024 * 1024


def iota(shape, dim):
    return lax.broadcasted_iota(I32, shape, dim)


def onehot(mask):
    return jnp.where(mask, 1.0, 0.0).astype(BF16)


def dot(a, b):
    return jnp.dot(a, b, preferred_element_type=F32)


def dot_t(a, b):
    return lax.dot_general(a, b, (((1,), (1,)), ((), ())), preferred_element_type=F32)


def face_row(face, kind):
    if kind == "xl":
        return 16 * (face >> 2) + (face & 3)
    if kind == "xh":
        return 16 * (face >> 2) + (face & 3) + 12
    if kind == "yl":
        return 4 * face
    return 4 * face + 3


def picker(kind):
    return onehot(iota((16, 64), 1) == face_row(iota((16, 64), 0), kind))


def spreader(kind):
    return onehot(iota((64, 16), 0) == face_row(iota((64, 16), 1), kind))


def side_weights(axis):
    here = lax.axis_index(axis)
    count = lax.axis_size(axis)
    odd = (here & 1).astype(F32)
    even = 1.0 - odd
    low = (here > 0).astype(F32)
    high = (here < count - 1).astype(F32)
    return odd, even, low, high


def pick_sides(first, second, axis):
    odd, even, low, high = side_weights(axis)
    first = first.astype(F32)
    second = second.astype(F32)
    below = (first * odd + second * even) * low
    above = (first * even + second * odd) * high
    return below.astype(BF16), above.astype(BF16)


def swap(cells, axis, offset):
    count = lax.axis_size(axis)
    pairs = [(i, (((i - offset) % count) ^ 1) + offset) for i in range(count)]
    return lax.ppermute(cells, axis, [(i, j % count) for i, j in pairs])


def exchange(sends):
    xa, xb, ya, yb = sends
    return swap(xa, "gx", 0), swap(xb, "gx", 1), swap(ya, "gy", 0), swap(yb, "gy", 1)


def shifted(block, step):
    lanes = iota((16, 128), 1)
    edge = 127 if step == 127 else 0
    return jnp.where(lanes == edge, 0.0, pltpu.roll(block.astype(F32), step, 1)).astype(BF16)


class Halo:
    def __init__(self, received):
        xa, xb, ya, yb = received
        left, right = pick_sides(xa[...], xb[...], "gx")
        down, up = pick_sides(ya[...], yb[...], "gy")
        self.left = dot(spreader("xh"), left).astype(BF16)
        self.right = dot(spreader("xl"), right).astype(BF16)
        self.down = dot(spreader("yh"), down).astype(BF16)
        self.up = dot(spreader("yl"), up).astype(BF16)


def neighbours(wb, halo, x, cells_x):
    own = wb[x]
    lanes = own.shape[1]
    after = wb[x + 1] if x + 1 < cells_x else halo.right
    before = wb[x - 1] if x > 0 else halo.left
    rows = iota((64, lanes), 0)
    along_x = jnp.where((rows & 12) == 0, after, before)
    here = slice(x * 128, (x + 1) * 128)
    after_y = jnp.concatenate([own[:, 128:], halo.up[:, here]], axis=1)
    before_y = jnp.concatenate([halo.down[:, here], own[:, :-128]], axis=1)
    along_y = jnp.where((rows & 3) == 0, after_y, before_y)
    blocks = [slice(b, b + 128) for b in range(0, lanes, 128)]
    z_low = jnp.concatenate([shifted(own[0:16, b], 127) for b in blocks], axis=1)
    z_high = jnp.concatenate([shifted(own[48:64, b], 1) for b in blocks], axis=1)
    return jnp.concatenate([own, along_x, along_y, z_low, z_high], axis=0)


def send_faces(rows, sends):
    xa, xb, ya, yb = sends
    odd, even, _, _ = side_weights("gx")
    x_low = dot(picker("xl"), rows(0))
    x_high = dot(picker("xh"), rows(7))
    xa[...] = (x_low * odd + x_high * even).astype(BF16)
    xb[...] = (x_low * even + x_high * odd).astype(BF16)
    odd, even, _, _ = side_weights("gy")
    both = jnp.concatenate([picker("yl"), picker("yh")], axis=0)
    for x in range(8):
        row = rows(x)
        ends = dot(both, jnp.concatenate([row[:, :128], row[:, -128:]], axis=1))
        y_low = ends[:16, :128]
        y_high = ends[16:, 128:]
        here = slice(x * 128, (x + 1) * 128)
        ya[:, here] = (y_low * odd + y_high * even).astype(BF16)
        yb[:, here] = (y_low * even + y_high * odd).astype(BF16)


def start_kernel(u, rhs, kappa, w, wb, rhs_p, xa, xb, ya, yb, stage):
    cells_x = kappa.shape[0]

    def load(source, scaled):
        def one(x, carry):
            scale = kappa[x]
            for q in range(64):
                tile = source[q, x].astype(F32)
                stage[pl.ds(pl.multiple_of(q * 64 + x * 8, 8), 8), :] = tile * scale if scaled else tile
            return carry

        lax.fori_loop(0, cells_x, one, 0)

    def gather(x, y):
        return [stage[pl.ds(k * 64 + x * 8 + y, 16, stride=256), :] for k in range(4)]

    load(u, True)

    def fill_w(x, carry):
        for y in range(8):
            for k, part in enumerate(gather(x, y)):
                w[x, 16 * k : 16 * k + 16, 128 * y : 128 * y + 128] = part
                wb[x, 16 * k : 16 * k + 16, 128 * y : 128 * y + 128] = part.astype(BF16)
        return carry

    lax.fori_loop(0, cells_x, fill_w, 0)
    send_faces(lambda x: wb[x], (xa, xb, ya, yb))
    load(rhs, False)

    def fill_rhs(x, carry):
        for y in range(8):
            for k, part in enumerate(gather(x, y)):
                rhs_p[x, 16 * k : 16 * k + 16, 128 * y : 128 * y + 128] = part.astype(BF16)
        return carry

    lax.fori_loop(0, cells_x, fill_rhs, 0)


def matrices_kernel(diag, coupling, smoother, restriction, sweep_matrix, rest_matrix, source_matrix):
    order = onehot(iota((64, 64), 1) == 4 * (iota((64, 64), 0) & 15) + (iota((64, 64), 0) >> 4))
    order_t = onehot(iota((64, 64), 0) == 4 * (iota((64, 64), 1) & 15) + (iota((64, 64), 1) >> 4))

    def place(rows, wanted):
        column = iota((rows, 256), 1)
        p = column & 63
        face, k, i, j = iota((rows, 256), 0), p >> 4, (p >> 2) & 3, p & 3
        return onehot(wanted(column >> 6, p, face, k, i, j))

    operator = dot(diag[...], place(64, lambda part, p, f, k, i, j: (part == 0) & (f == 4 * (p & 15) + k)))
    wanted = (
        lambda part, p, f, k, i, j: (part == 1) & (i == 0) & (f == 4 * j + k),
        lambda part, p, f, k, i, j: (part == 1) & (i == 3) & (f == 4 * j + k),
        lambda part, p, f, k, i, j: (part == 2) & (j == 0) & (f == 4 * i + k),
        lambda part, p, f, k, i, j: (part == 2) & (j == 3) & (f == 4 * i + k),
        lambda part, p, f, k, i, j: (part == 3) & (p == f),
        lambda part, p, f, k, i, j: (part == 3) & (p == f + 16),
    )
    for side in range(6):
        operator = operator + dot(coupling[side], place(16, wanted[side]))
    operator = operator.astype(BF16)
    ordered = dot(order, smoother[...]).astype(BF16)
    full = dot(ordered, operator)
    high = full.astype(BF16)
    sweep_matrix[0:64, :] = high
    sweep_matrix[64:128, :] = (full - high.astype(F32)).astype(BF16)
    full = dot(restriction[...], operator)
    high = full.astype(BF16)
    rest_matrix[...] = jnp.concatenate([high.astype(F32), full - high.astype(F32)], axis=0).astype(BF16)
    source_matrix[...] = jnp.concatenate(
        [dot(ordered, order_t), dot(restriction[...], order_t), jnp.zeros((8, 64), F32)], axis=0
    ).astype(BF16)


def first_kernel(w, wb, rhs_p, source_matrix, matrix, xa, xb, ya, yb, w_new, wb_new, c, cr, oxa, oxb, oya, oyb):
    halo = Halo((xa, xb, ya, yb))
    for x in range(8):
        source = dot(source_matrix[...], rhs_p[x])
        c[x] = source[0:64]
        cr[x] = source[64:72]
        change = dot(matrix[:, :224], neighbours(wb, halo, x, 8))
        new = w[x] + source[0:64] - (change[:64] + change[64:])
        w_new[x] = new
        wb_new[x] = new.astype(BF16)
    send_faces(lambda x: wb_new[x], (oxa, oxb, oya, oyb))


def sweep_kernel(w, wb, c, matrix, xa, xb, ya, yb, w_new, wb_new, oxa, oxb, oya, oyb):
    halo = Halo((xa, xb, ya, yb))
    for x in range(8):
        change = dot(matrix[:, :224], neighbours(wb, halo, x, 8))
        new = w[x] + c[x] - (change[:64] + change[64:])
        w_new[x] = new
        wb_new[x] = new.astype(BF16)
    send_faces(lambda x: wb_new[x], (oxa, oxb, oya, oyb))


def last_kernel(w, wb, c, matrix, kappa, xa, xb, ya, yb, out, stage):
    halo = Halo((xa, xb, ya, yb))
    for x in range(8):
        change = dot(matrix[:, :224], neighbours(wb, halo, x, 8))
        new = w[x] + c[x] - (change[:64] + change[64:])
        for y in range(8):
            for k in range(4):
                stage[pl.ds(k * 64 + x * 8 + y, 16, stride=256), :] = new[
                    16 * k : 16 * k + 16, 128 * y : 128 * y + 128
                ]

    def one(x, carry):
        scale = 1.0 / kappa[x]
        for q in range(64):
            out[q, x] = stage[pl.ds(pl.multiple_of(q * 64 + x * 8, 8), 8), :] * scale
        return carry

    lax.fori_loop(0, 8, one, 0)


def coarse_kernel(
    w, wb, cr, matrix, restriction_t, kappa, segment, blocks, xa, xb, ya, yb, w_new, wb_new, oxa, oxb, oya, oyb
):
    halo = Halo((xa, xb, ya, yb))
    numbers = iota((128, 128), 0)
    for x in range(8):
        change = dot(matrix[:, :224], neighbours(wb, halo, x, 8))
        restricted = cr[x] - (change[:8] + change[8:])
        for half in range(2):
            members = jnp.concatenate(
                [onehot(numbers == segment[x, y : y + 1, :] + 32 * (y & 3)) for y in range(4 * half, 4 * half + 4)],
                axis=1,
            )
            here = slice(512 * half, 512 * half + 512)
            weight = jnp.concatenate([kappa[x, y : y + 1, :] for y in range(4 * half, 4 * half + 4)], axis=1)
            fine = restricted[:, here]
            fine_high = fine.astype(BF16).astype(F32)
            one = weight.astype(BF16).astype(F32)
            two = (weight - one).astype(BF16).astype(F32)
            spare = iota((8, 512), 0)
            terms = jnp.where(spare == 0, one, jnp.where(spare == 1, two, jnp.where(spare == 2, weight - one - two, 0.0)))
            stack = jnp.concatenate([fine_high, fine - fine_high, terms, jnp.zeros((8, 512), F32)], axis=0)
            sums = dot_t(stack.astype(BF16), members)
            coarse = sums[0:8] + sums[8:16]
            total = sums[16:17] + sums[17:18] + sums[18:19]
            column = slice((2 * x + half) * 128, (2 * x + half) * 128 + 128)
            fix = jnp.concatenate(
                [jnp.sum(blocks[8 * p : 8 * p + 8, column] * coarse, axis=0, keepdims=True) for p in range(8)], axis=0
            )
            fix = fix / total
            fix_high = fix.astype(BF16).astype(F32)
            pair = jnp.concatenate([fix_high, fix - fix_high], axis=0).astype(BF16)
            spread = dot(pair, members).astype(BF16)
            correction = dot(restriction_t[...], spread)
            new = w[x, :, here] + correction * weight
            w_new[x, :, here] = new
            wb_new[x, :, here] = new.astype(BF16)
    send_faces(lambda x: wb_new[x], (oxa, oxb, oya, oyb))


def pack_kernel(inverse, places, out, stage):
    table = inverse[...].astype(BF16)
    numbers = iota((2048, 256), 0)
    for part in range(8):
        chosen = onehot(numbers == places[part])
        stage[:, 256 * part : 256 * part + 256] = dot(table, chosen)
    both = jnp.concatenate([stage[:, :1024], stage[:, 1024:]], axis=0)
    out[...] = jnp.transpose(both).reshape(128, 8, 128).astype(BF16)


def unpack_kernel(arrived, inverse, owner, out):
    here = lax.axis_index(("gx", "gy"))
    turned = jnp.transpose(arrived[...].astype(F32).reshape(1024, 128))
    table = jnp.concatenate([turned[:64], turned[64:]], axis=1).astype(BF16)
    earlier = onehot(iota((256, 256), 0) < iota((256, 256), 1))
    numbers = iota((2048, 256), 0)
    carry = jnp.zeros((128, 1), F32)
    for part in range(8):
        device = owner[part]
        hits = onehot(iota((128, 256), 0) == device)
        before = dot(hits, earlier) + carry
        hits = hits.astype(F32)
        rank = jnp.sum(hits * before, axis=0, keepdims=True).astype(I32)
        carry = carry + jnp.sum(hits, axis=1, keepdims=True)
        rank = jnp.minimum(rank, 15)
        slot = (rank >> 3) * 1024 + device * 8 + (rank & 7)
        mine = device == here
        far = dot(table, onehot(numbers == jnp.where(mine, -1, slot)))
        column = slice(256 * part, 256 * part + 256)
        out[:, column] = jnp.where(mine, inverse[:, column], far)


def run(body, ins, outs, scratch=()):
    return pl.pallas_call(
        body,
        out_shape=outs,
        in_specs=[pl.BlockSpec(memory_space=pltpu.VMEM)] * len(ins),
        out_specs=[pl.BlockSpec(memory_space=pltpu.VMEM)] * len(outs),
        scratch_shapes=list(scratch),
        compiler_params=pltpu.CompilerParams(vmem_limit_bytes=LIMIT),
    )(*ins)


def array(shape, dtype):
    return jax.ShapeDtypeStruct(shape, dtype)


def per_device(
    u_init, rhs, kappa, block_diagonal, face_coupling, smoother, restriction, coarse_inverse, segment_id, owner_device, arrival_place
):
    faces = [array((16, 1024), BF16)] * 4
    state = [array((8, 64, 1024), F32), array((8, 64, 1024), BF16)]
    inverse = coarse_inverse.reshape(64, 2048)
    places = arrival_place[0].reshape(128, 2, 8).transpose(1, 0, 2).reshape(8, 1, 256)
    (packed,) = run(pack_kernel, (inverse, places), [array((128, 8, 128), BF16)], [pltpu.VMEM((64, 2048), F32)])
    arrived = lax.all_to_all(packed, ("gx", "gy"), split_axis=0, concat_axis=0, tiled=True)
    owner = owner_device.reshape(8, 1, 256)
    (blocks,) = run(unpack_kernel, (arrived, inverse, owner), [array((64, 2048), F32)])

    matrix, rest_matrix, source_matrix = run(
        matrices_kernel,
        (block_diagonal, face_coupling, smoother, restriction),
        [array((128, 256), BF16), array((16, 256), BF16), array((80, 64), BF16)],
    )
    w, wb, rhs_p, *sends = run(
        start_kernel, (u_init, rhs, kappa), state + [array((8, 64, 1024), BF16)] + faces, [pltpu.VMEM((4096, 128), F32)]
    )
    w, wb, c, cr, *sends = run(
        first_kernel,
        (w, wb, rhs_p, source_matrix, matrix, *exchange(sends)),
        state + [array((8, 64, 1024), F32), array((8, 8, 1024), F32)] + faces,
    )
    for sweep_number in range(2):
        w, wb, *sends = run(sweep_kernel, (w, wb, c, matrix, *exchange(sends)), state + faces)
    back = jnp.transpose(restriction.reshape(8, 16, 4), (2, 1, 0)).reshape(64, 8)
    back = jnp.concatenate([back, back], axis=1)
    w, wb, *sends = run(
        coarse_kernel, (w, wb, cr, rest_matrix, back, kappa, segment_id, blocks, *exchange(sends)), state + faces
    )
    for sweep_number in range(2):
        w, wb, *sends = run(sweep_kernel, (w, wb, c, matrix, *exchange(sends)), state + faces)
    (out,) = run(
        last_kernel,
        (w, wb, c, matrix, kappa, *exchange(sends)),
        [array((64, 8, 8, 128), F32)],
        [pltpu.VMEM((4096, 128), F32)],
    )
    return out


def solution(mesh):
    return jax.shard_map(
        per_device,
        mesh=mesh,
        in_specs=(
            P(None, "gx", "gy", None),
            P(None, "gx", "gy", None),
            P("gx", "gy", None),
            P(),
            P(),
            P(),
            P(),
            P(None, None, ("gx", "gy")),
            P("gx", "gy", None),
            P("gx", "gy", None),
            P(("gx", "gy"), None, None),
        ),
        out_specs=P(None, "gx", "gy", None),
        check_vma=False,
    )
```

```python
import jax
import jax.numpy as jnp
from jax import lax
from jax.experimental import pallas as pl
from jax.experimental.pallas import tpu as pltpu
from jax.sharding import PartitionSpec as P


F32 = jnp.float32
BF16 = jnp.bfloat16
I32 = jnp.int32
LIMIT = 30 * 1024 * 1024


def iota(shape, dim):
    return lax.broadcasted_iota(I32, shape, dim)


def onehot(mask):
    return jnp.where(mask, 1.0, 0.0).astype(BF16)


def dot(a, b):
    return jnp.dot(a, b, preferred_element_type=F32)


def dot_t(a, b):
    return lax.dot_general(a, b, (((1,), (1,)), ((), ())), preferred_element_type=F32)


def face_row(face, kind):
    first, second = face >> 2, face & 3
    if kind == "xl":
        return 16 * second + first
    if kind == "xh":
        return 16 * second + first + 12
    if kind == "yl":
        return 16 * second + 4 * first
    return 16 * second + 4 * first + 3


def picker(kind):
    return onehot(iota((16, 64), 1) == face_row(iota((16, 64), 0), kind)).astype(F32)


def side_weights(axis):
    here = lax.axis_index(axis)
    count = lax.axis_size(axis)
    odd = (here & 1).astype(F32)
    even = 1.0 - odd
    low = (here > 0).astype(F32)
    high = (here < count - 1).astype(F32)
    return odd, even, low, high


def face_sender(axis, low_kind, high_kind):
    odd, even, _, _ = side_weights(axis)
    low, high = picker(low_kind), picker(high_kind)
    first = jnp.concatenate([low * odd, high * even], axis=1)
    second = jnp.concatenate([low * even, high * odd], axis=1)
    return jnp.concatenate([first, second], axis=0).astype(BF16)


def face_receiver(axis, below_matrix, above_matrix):
    odd, even, low, high = side_weights(axis)
    below = jnp.concatenate([below_matrix * (odd * low), below_matrix * (even * low)], axis=1)
    above = jnp.concatenate([above_matrix * (even * high), above_matrix * (odd * high)], axis=1)
    return jnp.concatenate([below, above], axis=0).astype(BF16)


def swap(cells, axis, offset):
    count = lax.axis_size(axis)
    pairs = [(i, (((i - offset) % count) ^ 1) + offset) for i in range(count)]
    return lax.ppermute(cells, axis, [(i, j % count) for i, j in pairs])


def exchange(sends):
    xa, xb, ya, yb = sends
    return swap(xa, "gx", 0), swap(xb, "gx", 1), swap(ya, "gy", 0), swap(yb, "gy", 1)


def shifted(block, step):
    lanes = iota((16, 128), 1)
    edge = 127 if step == 127 else 0
    return jnp.where(lanes == edge, 0.0, pltpu.roll(block.astype(F32), step, 1)).astype(BF16)


def neighbours(wb, x, cells_x):
    own = wb[x]
    lanes = own.shape[1]
    nothing = jnp.zeros_like(own)
    after = wb[x + 1] if x + 1 < cells_x else nothing
    before = wb[x - 1] if x > 0 else nothing
    rows = iota((64, lanes), 0)
    along_x = jnp.where((rows & 12) == 0, after, before)
    after_y = jnp.concatenate([own[:, 128:], nothing[:, :128]], axis=1)
    before_y = jnp.concatenate([nothing[:, :128], own[:, :-128]], axis=1)
    along_y = jnp.where((rows & 3) == 0, after_y, before_y)
    blocks = [slice(b, b + 128) for b in range(0, lanes, 128)]
    z_low = jnp.concatenate([shifted(own[0:16, b], 127) for b in blocks], axis=1)
    z_high = jnp.concatenate([shifted(own[48:64, b], 1) for b in blocks], axis=1)
    return jnp.concatenate([own, along_x, along_y, z_low, z_high], axis=0)


def side_changes(faces, received, rows):
    xa, xb, ya, yb = received
    out = []
    for axis, pair in ((0, (xa, xb)), (1, (ya, yb))):
        both = dot(faces[axis], jnp.concatenate([pair[0][...], pair[1][...]], axis=0))
        out += [both[0:rows] + both[rows : 2 * rows], both[2 * rows : 3 * rows] + both[3 * rows :]]
    return out


def send_faces(x_sender, y_sender, row, end, sends):
    xa, xb, ya, yb = sends
    both = dot(x_sender, jnp.concatenate([row(0), row(7)], axis=0)).astype(BF16)
    xa[...] = both[:16]
    xb[...] = both[16:]
    low = jnp.concatenate([end(x, slice(0, 128)) for x in range(8)], axis=1)
    high = jnp.concatenate([end(x, slice(896, 1024)) for x in range(8)], axis=1)
    both = dot(y_sender, jnp.concatenate([low, high], axis=0)).astype(BF16)
    ya[...] = both[:16]
    yb[...] = both[16:]


def to_lines(source, target, x):
    for k in range(4):
        for half in range(2):
            tiles = jnp.stack([source[4 * (8 * half + m) + k, x].astype(F32) for m in range(8)], axis=0)
            tiles = jnp.swapaxes(tiles, 0, 1)
            for y in range(8):
                target(16 * k + 8 * half, y, tiles[y])


def start_kernel(u_hbm, rhs_hbm, kappa_hbm, packed, u_out, rhs_out, *rest):
    faces_out, (u, rhs, kappa, u_p, rhs_p, xa, xb, ya, yb, in_sem, row_sem, face_sem) = rest[:4], rest[4:]
    loads = [
        pltpu.make_async_copy(source, target, in_sem.at[i])
        for i, (source, target) in enumerate(((u_hbm, u), (kappa_hbm, kappa), (rhs_hbm, rhs)))
    ]
    for copy in loads:
        copy.start()

    def row_copy(i, x):
        source, target = ((u_p, u_out), (rhs_p, rhs_out))[i]
        return pltpu.make_async_copy(source.at[x], target.at[x], row_sem.at[i, x])

    def relayout(i, source, lines):
        def body(x, carry):
            rows = {}

            def keep(p, y, tile):
                rows[p, y] = tile

            to_lines(source, keep, x)
            for p in range(0, 64, 16):
                for y in range(8):
                    both = jnp.concatenate([rows[p, y], rows[p + 8, y]], axis=0)
                    lines[x, p : p + 16, 128 * y : 128 * y + 128] = both.astype(BF16)
            row_copy(i, x).start()
            return carry

        lax.fori_loop(0, 8, body, 0)

    loads[0].wait()
    relayout(0, u, u_p)
    loads[1].wait()

    def line(x, y):
        return (u_p[x, :, 128 * y : 128 * y + 128].astype(F32) * kappa[x, y : y + 1, :]).astype(BF16)

    send_faces(
        face_sender("gx", "xl", "xh"),
        face_sender("gy", "yl", "yh"),
        lambda x: jnp.concatenate([line(x, y) for y in range(8)], axis=1),
        lambda x, lanes: line(x, lanes.start // 128),
        (xa, xb, ya, yb),
    )
    face_copies = [
        pltpu.make_async_copy(source, target, face_sem.at[i])
        for i, (source, target) in enumerate(zip((xa, xb, ya, yb), faces_out))
    ]
    for copy in face_copies:
        copy.start()
    loads[2].wait()
    relayout(1, rhs, rhs_p)

    def finish(x, carry):
        for i in range(2):
            row_copy(i, x).wait()
        return carry

    lax.fori_loop(0, 8, finish, 0)
    for copy in face_copies:
        copy.wait()


def split(full):
    high = full.astype(BF16).astype(F32)
    return jnp.concatenate([high, full - high], axis=0).astype(BF16)


def matrices_kernel(diag, coupling_t, smoother, restriction, arrived, matrix, rest, source, faces, rest_faces, senders, back):
    order = onehot(iota((64, 64), 1) == 4 * (iota((64, 64), 0) & 15) + (iota((64, 64), 0) >> 4))
    order_t = onehot(iota((64, 64), 0) == 4 * (iota((64, 64), 1) & 15) + (iota((64, 64), 1) >> 4))
    coupling = [jnp.transpose(coupling_t[side].astype(F32)).astype(BF16) for side in range(6)]

    def place(rows, wanted):
        column = iota((rows, 256), 1)
        p = column & 63
        face, k, i, j = iota((rows, 256), 0), p >> 4, (p >> 2) & 3, p & 3
        return onehot(wanted(column >> 6, p, face, k, i, j))

    operator = dot(diag[...], place(64, lambda part, p, f, k, i, j: (part == 0) & (f == 4 * (p & 15) + k)))
    wanted = (
        lambda part, p, f, k, i, j: (part == 1) & (i == 0) & (f == 4 * j + k),
        lambda part, p, f, k, i, j: (part == 1) & (i == 3) & (f == 4 * j + k),
        lambda part, p, f, k, i, j: (part == 2) & (j == 0) & (f == 4 * i + k),
        lambda part, p, f, k, i, j: (part == 2) & (j == 3) & (f == 4 * i + k),
        lambda part, p, f, k, i, j: (part == 3) & (p == f),
        lambda part, p, f, k, i, j: (part == 3) & (p == f + 16),
    )
    for side in range(6):
        operator = operator + dot(coupling[side], place(16, wanted[side]))
    operator = operator.astype(BF16)
    ordered = dot(order, smoother[...]).astype(BF16)
    matrix[...] = split(dot(ordered, operator))
    rest[...] = split(dot(restriction[...], operator))
    source[...] = jnp.concatenate(
        [dot(ordered, order_t), dot(restriction[...], order_t), jnp.zeros((8, 64), F32)], axis=0
    ).astype(BF16)
    one = [split(dot(ordered, coupling[side])).astype(F32) for side in range(4)]
    faces[0] = face_receiver("gx", one[1], one[0])
    faces[1] = face_receiver("gy", one[3], one[2])
    one = [split(dot(restriction[...], coupling[side])).astype(F32) for side in range(4)]
    rest_faces[0] = face_receiver("gx", one[1], one[0])
    rest_faces[1] = face_receiver("gy", one[3], one[2])
    senders[0] = face_sender("gx", "xl", "xh")
    senders[1] = face_sender("gy", "yl", "yh")
    twice = jnp.concatenate([restriction[...].astype(F32)] * 2, axis=0).astype(BF16)
    back[...] = dot_t(order, twice).astype(BF16)


def change_of(matrix, wb, x, rows):
    both = dot(matrix[:, :224], neighbours(wb, x, 8))
    return both[:rows] + both[rows:]


def first_inner_kernel(u_hbm, rhs_hbm, kappa, arrived, source_matrix, matrix, w_new, wb_new, c, cr, u_p, wb, rhs_p, sem):
    copies = [
        [
            pltpu.make_async_copy(source.at[x], target.at[x], sem.at[i, x])
            for i, (source, target) in enumerate(((u_hbm, u_p), (rhs_hbm, rhs_p)))
        ]
        for x in range(8)
    ]
    for row in copies:
        row[0].start()
    for row in copies:
        row[1].start()

    def scaled(x):
        copies[x][0].wait()
        for y in range(8):
            here = slice(128 * y, 128 * y + 128)
            w_new[x, :, here] = u_p[x, :, here].astype(F32) * kappa[x, y : y + 1, :]
            wb[x, :, here] = w_new[x, :, here].astype(BF16)

    for x in range(8):
        scaled(x)
    for x in range(8):
        copies[x][1].wait()
        source = dot(source_matrix[...], rhs_p[x])
        c[x] = source[0:64]
        cr[x] = source[64:72]
        new = w_new[x] + source[0:64] - change_of(matrix, wb, x, 64)
        w_new[x] = new
        wb_new[x] = new.astype(BF16)


def inner_kernel(w, wb, c, matrix, w_new, wb_new):
    for x in range(8):
        new = w[x] + c[x] - change_of(matrix, wb, x, 64)
        w_new[x] = new
        wb_new[x] = new.astype(BF16)


def add_sides(w_in, w, wb, faces, senders, received, sends):
    left, right, down, up = side_changes(faces, received, 64)
    for x in range(8):
        here = slice(x * 128, (x + 1) * 128)
        if x in (0, 7):
            edge = left if x == 0 else right
            first = edge[:, :128] + down[:, here]
            final = edge[:, -128:] + up[:, here]
            new = w_in[x] - jnp.concatenate([first, edge[:, 128:-128], final], axis=1)
            w[x] = new
            wb[x] = new.astype(BF16)
        else:
            for lanes, change in ((slice(0, 128), down), (slice(896, 1024), up)):
                new = w_in[x, :, lanes] - change[:, here]
                w[x, :, lanes] = new
                wb[x, :, lanes] = new.astype(BF16)
    send_faces(senders[0], senders[1], lambda x: wb[x], lambda x, lanes: wb[x, :, lanes], sends)


def sides_kernel(w_in, wb_in, faces, senders, after, xa, xb, ya, yb, w, wb, oxa, oxb, oya, oyb):
    add_sides(w_in, w, wb, faces, senders, (xa, xb, ya, yb), (oxa, oxb, oya, oyb))


def first_sides_kernel(w_in, wb_in, faces, senders, xa, xb, ya, yb, w, wb, oxa, oxb, oya, oyb, vxa, vxb, vya, vyb, sem):
    inside = (vxa, vxb, vya, vyb)
    copies = [pltpu.make_async_copy(s, t, sem.at[i]) for i, (s, t) in enumerate(zip((xa, xb, ya, yb), inside))]
    for copy in copies:
        copy.start()
    for copy in copies:
        copy.wait()
    add_sides(w_in, w, wb, faces, senders, inside, (oxa, oxb, oya, oyb))


def rest_kernel(wb, cr, rest, out):
    for x in range(8):
        out[x] = cr[x] - change_of(rest, wb, x, 8)


def line_mask(rows):
    return [(iota((rows, 128), 1) >> 5) == line for line in range(4)]


def members_kernel(segment, kappa, members, total):
    mask = line_mask(8)
    numbers = iota((32, 128), 0)
    spare = iota((8, 128), 0)
    for x in range(8):
        for half in range(2):
            group = 2 * x + half
            lines = range(4 * half, 4 * half + 4)
            hits = jnp.concatenate([onehot(numbers == segment[x, y : y + 1, :]) for y in lines], axis=0)
            members[group] = hits
            terms = []
            for y in lines:
                weight = kappa[x, y : y + 1, :]
                one = weight.astype(BF16).astype(F32)
                two = (weight - one).astype(BF16).astype(F32)
                last = weight - one - two
                terms.append(jnp.where(spare == 0, one, jnp.where(spare == 1, two, jnp.where(spare == 2, last, 0.0))))
            sums = dot_t(jnp.concatenate(terms, axis=0).astype(BF16), hits)
            kept = sum(jnp.where(mask[i], sums[8 * i : 8 * i + 8], 0.0) for i in range(4))
            total[group] = jnp.sum(kept, axis=0, keepdims=True)


def coarse_kernel(
    w, restricted, kappa, members, blocks, rest_faces, senders, back, xa, xb, ya, yb, w_new, wb_new, oxa, oxb, oya, oyb, coarse
):
    left, right, down, up = side_changes(rest_faces, (xa, xb, ya, yb), 8)
    mask = line_mask(8)
    for x in range(8):
        here = slice(x * 128, (x + 1) * 128)
        first, middle, final = down[:, here], jnp.zeros((8, 768), F32), up[:, here]
        if x in (0, 7):
            edge = left if x == 0 else right
            first, middle, final = first + edge[:, :128], edge[:, 128:-128], final + edge[:, -128:]
        fine = restricted[x] - jnp.concatenate([first, middle, final], axis=1)
        high = fine.astype(BF16).astype(F32)
        low = fine - high
        for half in range(2):
            group = 2 * x + half
            lanes = [slice(128 * y, 128 * y + 128) for y in range(4 * half, 4 * half + 4)]
            stack = jnp.concatenate([part[:, lane] for lane in lanes for part in (high, low)], axis=0)
            sums = dot_t(stack.astype(BF16), members[group])
            known = sum(
                jnp.where(mask[i], sums[16 * i : 16 * i + 8] + sums[16 * i + 8 : 16 * i + 16], 0.0) for i in range(4)
            )
            coarse[:, 128 * group : 128 * group + 128] = known
    known = coarse[...]
    fix = jnp.concatenate(
        [jnp.sum(blocks[8 * p : 8 * p + 8, :] * known, axis=0, keepdims=True) for p in range(8)], axis=0
    )
    high = fix.astype(BF16).astype(F32)
    low = fix - high
    for x in range(8):
        for half in range(2):
            group = 2 * x + half
            here = slice(512 * half, 512 * half + 512)
            lanes = slice(128 * group, 128 * group + 128)
            stack = jnp.concatenate(
                [jnp.where(mask[i], part[:, lanes], 0.0) for i in range(4) for part in (high, low)], axis=0
            )
            spread = dot(stack.astype(BF16), members[group]).astype(BF16)
            spread = jnp.concatenate([spread[16 * i : 16 * i + 16] for i in range(4)], axis=1)
            weight = jnp.concatenate([kappa[x, y : y + 1, :] for y in range(4 * half, 4 * half + 4)], axis=1)
            new = w[x, :, here] + dot(back[...], spread) * weight
            w_new[x, :, here] = new
            wb_new[x, :, here] = new.astype(BF16)
    send_faces(senders[0], senders[1], lambda x: wb_new[x], lambda x, lanes: wb_new[x, :, lanes], (oxa, oxb, oya, oyb))


def from_lines(x, line, store):
    for k in range(4):
        for half in range(2):
            rows = slice(16 * k + 8 * half, 16 * k + 8 * half + 8)
            tiles = jnp.swapaxes(jnp.stack([line(y)[rows] for y in range(8)], axis=0), 0, 1)
            for m in range(8):
                store(4 * (8 * half + m) + k, tiles[m])


def last_inner_kernel(w, wb, c, matrix, kappa, out):
    for x in range(8):
        new = w[x] + c[x] - change_of(matrix, wb, x, 64)
        scale = 1.0 / kappa[x]

        def store(q, tile):
            out[q, x] = tile * scale

        from_lines(x, lambda y: new[:, 128 * y : 128 * y + 128], store)


def last_sides_kernel(old, faces, kappa, xa, xb, ya, yb, out, new, sem):
    left, right, down, up = side_changes(faces, (xa, xb, ya, yb), 64)
    zero = jnp.zeros((64, 128), F32)
    copies = []
    for x in range(8):
        here = slice(x * 128, (x + 1) * 128)
        lines = [down[:, here]] + [zero] * 6 + [up[:, here]]
        if x in (0, 7):
            edge = left if x == 0 else right
            lines = [lines[y] + edge[:, 128 * y : 128 * y + 128] for y in range(8)]
        scale = 1.0 / kappa[x]

        def store(q, tile):
            new[q, x] = old[q, x] - tile * scale

        from_lines(x, lambda y: lines[y], store)
        copies.append(pltpu.make_async_copy(new.at[:, x], out.at[:, x], sem.at[x]))
        copies[-1].start()
    for copy in copies:
        copy.wait()


def pack_kernel(inverse_hbm, places_hbm, out, stage, inverse, places, sem):
    copies = [pltpu.make_async_copy(inverse_hbm, inverse, sem.at[0]), pltpu.make_async_copy(places_hbm, places, sem.at[1])]
    for copy in copies:
        copy.start()
    for copy in copies:
        copy.wait()
    table = inverse[...].astype(BF16)
    numbers = iota((2048, 256), 0)
    for r in range(8):
        wanted = jnp.concatenate([places[r : r + 1, :], places[r + 8 : r + 9, :]], axis=1)
        chosen = dot(table, onehot(numbers == wanted))
        both = jnp.concatenate([chosen[:, :128], chosen[:, 128:]], axis=0)
        stage[pl.ds(r, 128, stride=8), :] = jnp.transpose(both)
    out[...] = stage[...].reshape(128, 8, 128).astype(BF16)


def unpack_kernel(arrived, inverse, owner, total, out):
    here = lax.axis_index(("gx", "gy"))
    turned = jnp.transpose(arrived[...].astype(F32).reshape(1024, 128))
    table = jnp.concatenate([turned[:64], turned[64:]], axis=1).astype(BF16)
    earlier = onehot(iota((256, 256), 0) < iota((256, 256), 1))
    repeat = onehot(iota((32, 256), 0) == (iota((32, 256), 1) & 31))
    of_line = iota((8, 256), 0) == (iota((8, 256), 1) >> 5)
    numbers = iota((2048, 256), 0)
    carry = jnp.zeros((128, 1), F32)
    for x in range(8):
        repeated = dot(owner[x].astype(F32).astype(BF16), repeat)
        device = jnp.sum(jnp.where(of_line, repeated, 0.0), axis=0, keepdims=True).astype(I32)
        hits = onehot(iota((128, 256), 0) == device)
        before = dot(hits, earlier) + carry
        hits = hits.astype(F32)
        rank = jnp.sum(hits * before, axis=0, keepdims=True).astype(I32)
        carry = carry + jnp.sum(hits, axis=1, keepdims=True)
        rank = jnp.minimum(rank, 15)
        slot = (rank >> 3) * 1024 + device * 8 + (rank & 7)
        mine = device == here
        far = dot(table, onehot(numbers == jnp.where(mine, -1, slot)))
        column = slice(256 * x, 256 * x + 256)
        weight = jnp.concatenate([total[2 * x], total[2 * x + 1]], axis=1)
        out[:, column] = jnp.where(mine, inverse[:, column], far) / weight


VMEM_SPEC = pl.BlockSpec(memory_space=pltpu.VMEM)
HBM_SPEC = pl.BlockSpec(memory_space=pl.ANY)


def run(body, ins, outs, scratch=(), in_hbm=(), out_hbm=(), anywhere=(), aliases=None):
    ins = [pltpu.with_memory_space_constraint(x, pltpu.HBM) if i in in_hbm else x for i, x in enumerate(ins)]
    outs = [pltpu.HBM(x.shape, x.dtype) if i in out_hbm else x for i, x in enumerate(outs)]
    return pl.pallas_call(
        body,
        out_shape=outs,
        in_specs=[HBM_SPEC if i in in_hbm or i in anywhere else VMEM_SPEC for i in range(len(ins))],
        out_specs=[HBM_SPEC if i in out_hbm else VMEM_SPEC for i in range(len(outs))],
        scratch_shapes=list(scratch),
        input_output_aliases=aliases or {},
        compiler_params=pltpu.CompilerParams(vmem_limit_bytes=LIMIT),
    )(*ins)


def array(shape, dtype):
    return jax.ShapeDtypeStruct(shape, dtype)


def per_device(
    u_init, rhs, kappa, block_diagonal, face_coupling, smoother, restriction, coarse_inverse, segment_id, owner_device, arrival_place
):
    faces_shape = [array((16, 1024), BF16)] * 4
    state = [array((8, 64, 1024), F32), array((8, 64, 1024), BF16)]
    inverse = coarse_inverse.reshape(64, 2048)
    places = jnp.transpose(arrival_place[0])
    coupling_t = jnp.transpose(face_coupling, (0, 2, 1))

    (packed,) = run(
        pack_kernel,
        (inverse, places),
        [array((128, 8, 128), BF16)],
        [
            pltpu.VMEM((1024, 128), F32),
            pltpu.VMEM((64, 2048), F32),
            pltpu.VMEM((16, 128), I32),
            pltpu.SemaphoreType.DMA((2,)),
        ],
        in_hbm=(0, 1),
    )
    arrived = lax.all_to_all(packed, ("gx", "gy"), split_axis=0, concat_axis=0, tiled=True)
    lines = array((8, 64, 1024), BF16)
    lines_scratch = pltpu.VMEM((8, 64, 1024), BF16)
    u_p, rhs_p, *sends = run(
        start_kernel,
        (u_init, rhs, kappa, packed),
        [lines, lines] + faces_shape,
        [pltpu.VMEM((64, 8, 8, 128), BF16)] * 2
        + [pltpu.VMEM((8, 8, 128), F32)]
        + [pltpu.VMEM((8, 64, 1024), BF16)] * 2
        + [pltpu.VMEM((16, 1024), BF16)] * 4
        + [pltpu.SemaphoreType.DMA((3,)), pltpu.SemaphoreType.DMA((2, 8)), pltpu.SemaphoreType.DMA((4,))],
        in_hbm=(0, 1, 2, 3),
        out_hbm=range(6),
    )
    received = exchange(sends)
    matrix, rest, source_matrix, faces, rest_faces, senders, back = run(
        matrices_kernel,
        (block_diagonal, coupling_t, smoother, restriction, arrived),
        in_hbm=(4,),
        outs=[
            array((128, 256), BF16),
            array((16, 256), BF16),
            array((80, 64), BF16),
            array((2, 256, 32), BF16),
            array((2, 32, 32), BF16),
            array((2, 32, 128), BF16),
            array((64, 16), BF16),
        ],
    )
    w, wb, c, cr = run(
        first_inner_kernel,
        (u_p, rhs_p, kappa, arrived, source_matrix, matrix),
        state + [array((8, 64, 1024), F32), array((8, 8, 1024), F32)],
        [lines_scratch] * 3 + [pltpu.SemaphoreType.DMA((2, 8))],
        in_hbm=(0, 1, 3),
    )
    members, total = run(
        members_kernel, (segment_id, kappa), [array((16, 128, 128), BF16), array((16, 1, 128), F32)]
    )
    (blocks,) = run(unpack_kernel, (arrived, inverse, owner_device, total), [array((64, 2048), F32)])

    def sides(w, wb, received, after):
        w, wb, *sends = run(
            sides_kernel,
            (w, wb, faces, senders, after, *received),
            state + faces_shape,
            anywhere=(4,),
            aliases={0: 0, 1: 1},
        )
        return w, wb, exchange(sends)

    w, wb, *sends = run(
        first_sides_kernel,
        (w, wb, faces, senders, *received),
        state + faces_shape,
        [pltpu.VMEM((16, 1024), BF16)] * 4 + [pltpu.SemaphoreType.DMA((4,))],
        in_hbm=(4, 5, 6, 7),
        aliases={0: 0, 1: 1},
    )
    received = exchange(sends)
    for after in (members, blocks):
        w, wb = run(inner_kernel, (w, wb, c, matrix), state)
        w, wb, received = sides(w, wb, received, after)
    (restricted,) = run(rest_kernel, (wb, cr, rest), [array((8, 8, 1024), F32)])
    w, wb, *sends = run(
        coarse_kernel,
        (w, restricted, kappa, members, blocks, rest_faces, senders, back, *received),
        state + faces_shape,
        [pltpu.VMEM((8, 2048), F32)],
    )
    received = exchange(sends)
    for sweep_number in range(2):
        w, wb = run(inner_kernel, (w, wb, c, matrix), state)
        w, wb, received = sides(w, wb, received, members)
    (out,) = run(last_inner_kernel, (w, wb, c, matrix, kappa), [array((64, 8, 8, 128), F32)])
    (out,) = run(
        last_sides_kernel,
        (out, faces, kappa, *received),
        [array((64, 8, 8, 128), F32)],
        [pltpu.VMEM((64, 8, 8, 128), F32), pltpu.SemaphoreType.DMA((8,))],
        out_hbm=(0,),
    )
    return out


def solution(mesh):
    return jax.shard_map(
        per_device,
        mesh=mesh,
        in_specs=(
            P(None, "gx", "gy", None),
            P(None, "gx", "gy", None),
            P("gx", "gy", None),
            P(),
            P(),
            P(),
            P(),
            P(None, None, ("gx", "gy")),
            P("gx", "gy", None),
            P("gx", "gy", None),
            P(("gx", "gy"), None, None),
        ),
        out_specs=P(None, "gx", "gy", None),
        check_vma=False,
    )
```

```python
import jax
import jax.numpy as jnp
from jax import lax
from jax.experimental import pallas as pl
from jax.experimental.pallas import tpu as pltpu
from jax.sharding import PartitionSpec as P


F32 = jnp.float32
BF16 = jnp.bfloat16
I32 = jnp.int32
LIMIT = 30 * 1024 * 1024


def iota(shape, dim):
    return lax.broadcasted_iota(I32, shape, dim)


def onehot(mask):
    return jnp.where(mask, 1.0, 0.0).astype(BF16)


def dot(a, b):
    return jnp.dot(a, b, preferred_element_type=F32)


def dot_t(a, b):
    return lax.dot_general(a, b, (((1,), (1,)), ((), ())), preferred_element_type=F32)


def face_row(face, kind):
    first, second = face >> 2, face & 3
    if kind == "xl":
        return 16 * second + first
    if kind == "xh":
        return 16 * second + first + 12
    if kind == "yl":
        return 16 * second + 4 * first
    return 16 * second + 4 * first + 3


def picker(kind):
    return onehot(iota((16, 64), 1) == face_row(iota((16, 64), 0), kind)).astype(F32)


def side_weights(axis):
    here = lax.axis_index(axis)
    count = lax.axis_size(axis)
    odd = (here & 1).astype(F32)
    even = 1.0 - odd
    low = (here > 0).astype(F32)
    high = (here < count - 1).astype(F32)
    return odd, even, low, high


def face_sender(axis, low_kind, high_kind):
    odd, even, _, _ = side_weights(axis)
    low, high = picker(low_kind), picker(high_kind)
    first = jnp.concatenate([low * odd, high * even], axis=1)
    second = jnp.concatenate([low * even, high * odd], axis=1)
    return jnp.concatenate([first, second], axis=0).astype(BF16)


def face_receiver(axis, below_matrix, above_matrix):
    odd, even, low, high = side_weights(axis)
    below = jnp.concatenate([below_matrix * (odd * low), below_matrix * (even * low)], axis=1)
    above = jnp.concatenate([above_matrix * (even * high), above_matrix * (odd * high)], axis=1)
    return jnp.concatenate([below, above], axis=0).astype(BF16)


def swap(cells, axis, offset):
    count = lax.axis_size(axis)
    pairs = [(i, (((i - offset) % count) ^ 1) + offset) for i in range(count)]
    return lax.ppermute(cells, axis, [(i, j % count) for i, j in pairs])


def exchange(sends):
    xa, xb, ya, yb = sends
    return swap(xa, "gx", 0), swap(xb, "gx", 1), swap(ya, "gy", 0), swap(yb, "gy", 1)


def shifted(block, step):
    lanes = iota((16, 128), 1)
    edge = 127 if step == 127 else 0
    return jnp.where(lanes == edge, 0.0, pltpu.roll(block.astype(F32), step, 1)).astype(BF16)


def neighbours(wb, x, cells_x):
    own = wb[x]
    lanes = own.shape[1]
    nothing = jnp.zeros_like(own)
    after = wb[x + 1] if x + 1 < cells_x else nothing
    before = wb[x - 1] if x > 0 else nothing
    rows = iota((64, lanes), 0)
    along_x = jnp.where((rows & 12) == 0, after, before)
    after_y = jnp.concatenate([own[:, 128:], nothing[:, :128]], axis=1)
    before_y = jnp.concatenate([nothing[:, :128], own[:, :-128]], axis=1)
    along_y = jnp.where((rows & 3) == 0, after_y, before_y)
    blocks = [slice(b, b + 128) for b in range(0, lanes, 128)]
    z_low = jnp.concatenate([shifted(own[0:16, b], 127) for b in blocks], axis=1)
    z_high = jnp.concatenate([shifted(own[48:64, b], 1) for b in blocks], axis=1)
    return jnp.concatenate([own, along_x, along_y, z_low, z_high], axis=0)


def side_changes(faces, received, rows):
    xa, xb, ya, yb = received
    out = []
    for axis, pair in ((0, (xa, xb)), (1, (ya, yb))):
        both = dot(faces[axis], jnp.concatenate([pair[0][...], pair[1][...]], axis=0))
        out += [both[0:rows] + both[rows : 2 * rows], both[2 * rows : 3 * rows] + both[3 * rows :]]
    return out


def send_faces(x_sender, y_sender, row, end, sends):
    xa, xb, ya, yb = sends
    both = dot(x_sender, jnp.concatenate([row(0), row(7)], axis=0)).astype(BF16)
    xa[...] = both[:16]
    xb[...] = both[16:]
    low = jnp.concatenate([end(x, slice(0, 128)) for x in range(8)], axis=1)
    high = jnp.concatenate([end(x, slice(896, 1024)) for x in range(8)], axis=1)
    both = dot(y_sender, jnp.concatenate([low, high], axis=0)).astype(BF16)
    ya[...] = both[:16]
    yb[...] = both[16:]


def to_lines(source, target, x):
    for k in range(4):
        for half in range(2):
            tiles = jnp.stack([source[4 * (8 * half + m) + k, x].astype(F32) for m in range(8)], axis=0)
            tiles = jnp.swapaxes(tiles, 0, 1)
            for y in range(8):
                target(16 * k + 8 * half, y, tiles[y])


def start_kernel(u_hbm, rhs_hbm, kappa_hbm, packed, u_out, rhs_out, *rest):
    faces_out, (u, rhs, kappa, u_p, rhs_p, xa, xb, ya, yb, in_sem, row_sem, face_sem) = rest[:4], rest[4:]
    loads = [
        pltpu.make_async_copy(source, target, in_sem.at[i])
        for i, (source, target) in enumerate(((u_hbm, u), (kappa_hbm, kappa), (rhs_hbm, rhs)))
    ]
    for copy in loads:
        copy.start()

    def row_copy(i, x):
        source, target = ((u_p, u_out), (rhs_p, rhs_out))[i]
        return pltpu.make_async_copy(source.at[x], target.at[x], row_sem.at[i, x])

    def relayout(i, source, lines):
        def body(x, carry):
            rows = {}

            def keep(p, y, tile):
                rows[p, y] = tile

            to_lines(source, keep, x)
            for p in range(0, 64, 16):
                for y in range(8):
                    both = jnp.concatenate([rows[p, y], rows[p + 8, y]], axis=0)
                    lines[x, p : p + 16, 128 * y : 128 * y + 128] = both.astype(BF16)
            row_copy(i, x).start()
            return carry

        lax.fori_loop(0, 8, body, 0)

    loads[0].wait()
    relayout(0, u, u_p)
    loads[1].wait()

    def line(x, y):
        return (u_p[x, :, 128 * y : 128 * y + 128].astype(F32) * kappa[x, y : y + 1, :]).astype(BF16)

    send_faces(
        face_sender("gx", "xl", "xh"),
        face_sender("gy", "yl", "yh"),
        lambda x: jnp.concatenate([line(x, y) for y in range(8)], axis=1),
        lambda x, lanes: line(x, lanes.start // 128),
        (xa, xb, ya, yb),
    )
    face_copies = [
        pltpu.make_async_copy(source, target, face_sem.at[i])
        for i, (source, target) in enumerate(zip((xa, xb, ya, yb), faces_out))
    ]
    for copy in face_copies:
        copy.start()
    loads[2].wait()
    relayout(1, rhs, rhs_p)

    def finish(x, carry):
        for i in range(2):
            row_copy(i, x).wait()
        return carry

    lax.fori_loop(0, 8, finish, 0)
    for copy in face_copies:
        copy.wait()


def split(full):
    high = full.astype(BF16).astype(F32)
    return jnp.concatenate([high, full - high], axis=0).astype(BF16)


def make_matrices(diag, coupling_t, smoother, restriction, matrix, rest, source, faces, rest_faces, senders, back):
    order = onehot(iota((64, 64), 1) == 4 * (iota((64, 64), 0) & 15) + (iota((64, 64), 0) >> 4))
    order_t = onehot(iota((64, 64), 0) == 4 * (iota((64, 64), 1) & 15) + (iota((64, 64), 1) >> 4))
    coupling = [jnp.transpose(coupling_t[side].astype(F32)).astype(BF16) for side in range(6)]

    def place(rows, wanted):
        column = iota((rows, 256), 1)
        p = column & 63
        face, k, i, j = iota((rows, 256), 0), p >> 4, (p >> 2) & 3, p & 3
        return onehot(wanted(column >> 6, p, face, k, i, j))

    operator = dot(diag[...], place(64, lambda part, p, f, k, i, j: (part == 0) & (f == 4 * (p & 15) + k)))
    wanted = (
        lambda part, p, f, k, i, j: (part == 1) & (i == 0) & (f == 4 * j + k),
        lambda part, p, f, k, i, j: (part == 1) & (i == 3) & (f == 4 * j + k),
        lambda part, p, f, k, i, j: (part == 2) & (j == 0) & (f == 4 * i + k),
        lambda part, p, f, k, i, j: (part == 2) & (j == 3) & (f == 4 * i + k),
        lambda part, p, f, k, i, j: (part == 3) & (p == f),
        lambda part, p, f, k, i, j: (part == 3) & (p == f + 16),
    )
    for side in range(6):
        operator = operator + dot(coupling[side], place(16, wanted[side]))
    operator = operator.astype(BF16)
    ordered = dot(order, smoother[...]).astype(BF16)
    matrix[...] = split(dot(ordered, operator))
    rest[...] = split(dot(restriction[...], operator))
    source[...] = jnp.concatenate(
        [dot(ordered, order_t), dot(restriction[...], order_t), jnp.zeros((8, 64), F32)], axis=0
    ).astype(BF16)
    one = [split(dot(ordered, coupling[side])).astype(F32) for side in range(4)]
    faces[0] = face_receiver("gx", one[1], one[0])
    faces[1] = face_receiver("gy", one[3], one[2])
    one = [split(dot(restriction[...], coupling[side])).astype(F32) for side in range(4)]
    rest_faces[0] = face_receiver("gx", one[1], one[0])
    rest_faces[1] = face_receiver("gy", one[3], one[2])
    senders[0] = face_sender("gx", "xl", "xh")
    senders[1] = face_sender("gy", "yl", "yh")
    twice = jnp.concatenate([restriction[...].astype(F32)] * 2, axis=0).astype(BF16)
    back[...] = dot_t(order, twice).astype(BF16)


def change_of(matrix, wb, x, rows):
    both = dot(matrix[:, :224], neighbours(wb, x, 8))
    return both[:rows] + both[rows:]


def first_inner_kernel(
    u_hbm, rhs_hbm, kappa_hbm, arrived, diag, coupling_t, smoother, restriction, *rest_refs
):
    outs, (w_new, wb_new, c, cr), scratch = rest_refs[:6], rest_refs[6:10], rest_refs[10:]
    source_matrix, u_p, wb, rhs_p, kappa, sem, kappa_sem = scratch
    matrix, rest, faces, rest_faces, senders, back = outs

    def row_copy(i, x):
        source, target = ((u_hbm, u_p), (rhs_hbm, rhs_p))[i]
        return pltpu.make_async_copy(source.at[x], target.at[x], sem.at[i, x])

    copies = [[row_copy(i, x) for i in range(2)] for x in range(8)]
    kappa_copy = pltpu.make_async_copy(kappa_hbm, kappa, kappa_sem)
    kappa_copy.start()
    for row in copies:
        row[0].start()
        row[1].start()
    make_matrices(diag, coupling_t, smoother, restriction, matrix, rest, source_matrix, faces, rest_faces, senders, back)
    kappa_copy.wait()

    def scaled(x):
        copies[x][0].wait()
        for y in range(8):
            here = slice(128 * y, 128 * y + 128)
            value = u_p[x, :, here].astype(F32) * kappa[x, y : y + 1, :]
            w_new[x, :, here] = value
            wb[x, :, here] = value.astype(BF16)

    scaled(0)
    for x in range(8):
        if x < 7:
            scaled(x + 1)
        copies[x][1].wait()
        source = dot(source_matrix[...], rhs_p[x])
        c[x] = source[0:64]
        cr[x] = source[64:72]
        new = w_new[x] + source[0:64] - change_of(matrix, wb, x, 64)
        w_new[x] = new
        wb_new[x] = new.astype(BF16)


def inner_kernel(w, wb, c, matrix, w_new, wb_new):
    for x in range(8):
        new = w[x] + c[x] - change_of(matrix, wb, x, 64)
        w_new[x] = new
        wb_new[x] = new.astype(BF16)


def add_sides(w_in, w, wb, faces, senders, received, sends):
    left, right, down, up = side_changes(faces, received, 64)
    for x in range(8):
        here = slice(x * 128, (x + 1) * 128)
        if x in (0, 7):
            edge = left if x == 0 else right
            first = edge[:, :128] + down[:, here]
            final = edge[:, -128:] + up[:, here]
            new = w_in[x] - jnp.concatenate([first, edge[:, 128:-128], final], axis=1)
            w[x] = new
            wb[x] = new.astype(BF16)
        else:
            for lanes, change in ((slice(0, 128), down), (slice(896, 1024), up)):
                new = w_in[x, :, lanes] - change[:, here]
                w[x, :, lanes] = new
                wb[x, :, lanes] = new.astype(BF16)
    send_faces(senders[0], senders[1], lambda x: wb[x], lambda x, lanes: wb[x, :, lanes], sends)


def sides_kernel(w_in, wb_in, faces, senders, after, xa, xb, ya, yb, w, wb, oxa, oxb, oya, oyb):
    add_sides(w_in, w, wb, faces, senders, (xa, xb, ya, yb), (oxa, oxb, oya, oyb))


def first_sides_kernel(w_in, wb_in, faces, senders, xa, xb, ya, yb, w, wb, oxa, oxb, oya, oyb, vxa, vxb, vya, vyb, sem):
    inside = (vxa, vxb, vya, vyb)
    copies = [pltpu.make_async_copy(s, t, sem.at[i]) for i, (s, t) in enumerate(zip((xa, xb, ya, yb), inside))]
    for copy in copies:
        copy.start()
    for copy in copies:
        copy.wait()
    add_sides(w_in, w, wb, faces, senders, inside, (oxa, oxb, oya, oyb))


def rest_kernel(wb, cr, rest, out):
    for x in range(8):
        out[x] = cr[x] - change_of(rest, wb, x, 8)


def line_mask(rows):
    return [(iota((rows, 128), 1) >> 5) == line for line in range(4)]


def members_kernel(segment, kappa, owner, members, members_t, total, slots):
    mask = line_mask(8)
    numbers = iota((32, 128), 0)
    spare = iota((8, 128), 0)
    for x in range(8):
        for half in range(2):
            group = 2 * x + half
            lines = range(4 * half, 4 * half + 4)
            hits = jnp.concatenate([onehot(numbers == segment[x, y : y + 1, :]) for y in lines], axis=0)
            members[group] = hits
            members_t[group] = jnp.transpose(hits.astype(F32)).astype(BF16)
            terms = []
            for y in lines:
                weight = kappa[x, y : y + 1, :]
                one = weight.astype(BF16).astype(F32)
                two = (weight - one).astype(BF16).astype(F32)
                last = weight - one - two
                terms.append(jnp.where(spare == 0, one, jnp.where(spare == 1, two, jnp.where(spare == 2, last, 0.0))))
            sums = dot_t(jnp.concatenate(terms, axis=0).astype(BF16), hits)
            kept = sum(jnp.where(mask[i], sums[8 * i : 8 * i + 8], 0.0) for i in range(4))
            total[group] = jnp.sum(kept, axis=0, keepdims=True)
    here = lax.axis_index(("gx", "gy"))
    earlier = onehot(iota((256, 256), 0) < iota((256, 256), 1))
    repeat = onehot(iota((32, 256), 0) == (iota((32, 256), 1) & 31))
    of_line = iota((8, 256), 0) == (iota((8, 256), 1) >> 5)
    carry = jnp.zeros((128, 1), F32)
    for x in range(8):
        repeated = dot(owner[x].astype(F32).astype(BF16), repeat)
        device = jnp.sum(jnp.where(of_line, repeated, 0.0), axis=0, keepdims=True).astype(I32)
        hits = onehot(iota((128, 256), 0) == device)
        before = dot(hits, earlier) + carry
        hits = hits.astype(F32)
        rank = jnp.sum(hits * before, axis=0, keepdims=True).astype(I32)
        carry = carry + jnp.sum(hits, axis=1, keepdims=True)
        rank = jnp.minimum(rank, 15)
        slot = (rank >> 3) * 1024 + device * 8 + (rank & 7)
        slots[x] = jnp.where(device == here, -1, slot)


def coarse_kernel(
    w, restricted, kappa, members, members_t, blocks, rest_faces, senders, back, xa, xb, ya, yb, fix_out, oxa, oxb, oya, oyb, coarse
):
    left, right, down, up = side_changes(rest_faces, (xa, xb, ya, yb), 8)
    mask = line_mask(8)
    for x in range(8):
        here = slice(x * 128, (x + 1) * 128)
        first, middle, final = down[:, here], jnp.zeros((8, 768), F32), up[:, here]
        if x in (0, 7):
            edge = left if x == 0 else right
            first, middle, final = first + edge[:, :128], edge[:, 128:-128], final + edge[:, -128:]
        fine = restricted[x] - jnp.concatenate([first, middle, final], axis=1)
        high = fine.astype(BF16).astype(F32)
        low = fine - high
        for half in range(2):
            group = 2 * x + half
            lanes = [slice(128 * y, 128 * y + 128) for y in range(4 * half, 4 * half + 4)]
            stack = jnp.concatenate([part[:, lane] for lane in lanes for part in (high, low)], axis=0)
            sums = dot(stack.astype(BF16), members_t[group])
            known = sum(
                jnp.where(mask[i], sums[16 * i : 16 * i + 8] + sums[16 * i + 8 : 16 * i + 16], 0.0) for i in range(4)
            )
            coarse[:, 128 * group : 128 * group + 128] = known
    known = coarse[...]
    fix = jnp.concatenate(
        [jnp.sum(blocks[8 * p : 8 * p + 8, :] * known, axis=0, keepdims=True) for p in range(8)], axis=0
    )
    fix_out[...] = fix
    high = fix.astype(BF16).astype(F32)
    low = fix - high

    def spread_lines(x, wanted):
        out = {}
        for half in range(2):
            group = 2 * x + half
            lanes = slice(128 * group, 128 * group + 128)
            lines = [i for i in range(4) if 4 * half + i in wanted]
            stack = jnp.concatenate(
                [jnp.where(mask[i], part[:, lanes], 0.0) for i in lines for part in (high, low)], axis=0
            )
            spread = dot(stack.astype(BF16), members[group]).astype(BF16)
            for n, i in enumerate(lines):
                out[4 * half + i] = spread[16 * n : 16 * n + 16]
        return out

    def corrected(lines):
        spread = jnp.concatenate([spreads[x][y] for x, y in lines], axis=1)
        weight = jnp.concatenate([kappa[x, y : y + 1, :] for x, y in lines], axis=1)
        old = jnp.concatenate([w[x, :, 128 * y : 128 * y + 128] for x, y in lines], axis=1)
        return (old + dot(back[...], spread) * weight).astype(BF16)

    spreads = [spread_lines(x, range(8) if x in (0, 7) else (0, 7)) for x in range(8)]
    rows = {x: corrected([(x, y) for y in range(8)]) for x in (0, 7)}
    ends = {y: corrected([(x, y) for x in range(1, 7)]) for y in (0, 7)}

    def end(x, lanes):
        if x in rows:
            return rows[x][:, lanes]
        return ends[lanes.start // 128][:, 128 * (x - 1) : 128 * x]

    send_faces(senders[0], senders[1], lambda x: rows[x], end, (oxa, oxb, oya, oyb))


def corrected_inner_kernel(w, fix, kappa, members, back, c, matrix, w_new, wb_new, wb):
    mask = line_mask(8)
    high = fix[...].astype(BF16).astype(F32)
    low = fix[...] - high
    for x in range(8):
        for half in range(2):
            group = 2 * x + half
            here = slice(512 * half, 512 * half + 512)
            lanes = slice(128 * group, 128 * group + 128)
            stack = jnp.concatenate(
                [jnp.where(mask[i], part[:, lanes], 0.0) for i in range(4) for part in (high, low)], axis=0
            )
            spread = dot(stack.astype(BF16), members[group]).astype(BF16)
            spread = jnp.concatenate([spread[16 * i : 16 * i + 16] for i in range(4)], axis=1)
            weight = jnp.concatenate([kappa[x, y : y + 1, :] for y in range(4 * half, 4 * half + 4)], axis=1)
            new = w[x, :, here] + dot(back[...], spread) * weight
            w_new[x, :, here] = new
            wb[x, :, here] = new.astype(BF16)
    for x in range(8):
        new = w_new[x] + c[x] - change_of(matrix, wb, x, 64)
        w_new[x] = new
        wb_new[x] = new.astype(BF16)


def from_lines(x, line, store):
    for k in range(4):
        for half in range(2):
            rows = slice(16 * k + 8 * half, 16 * k + 8 * half + 8)
            tiles = jnp.swapaxes(jnp.stack([line(y)[rows] for y in range(8)], axis=0), 0, 1)
            for m in range(8):
                store(4 * (8 * half + m) + k, tiles[m])


def last_inner_kernel(w, wb, c, matrix, kappa, out):
    for x in range(8):
        new = w[x] + c[x] - change_of(matrix, wb, x, 64)
        scale = 1.0 / kappa[x]

        def store(q, tile):
            out[q, x] = tile * scale

        from_lines(x, lambda y: new[:, 128 * y : 128 * y + 128], store)


def last_sides_kernel(old, faces, kappa, xa, xb, ya, yb, out, new, sem):
    left, right, down, up = side_changes(faces, (xa, xb, ya, yb), 64)
    zero = jnp.zeros((64, 128), F32)
    copies = []
    for x in range(8):
        here = slice(x * 128, (x + 1) * 128)
        lines = [down[:, here]] + [zero] * 6 + [up[:, here]]
        if x in (0, 7):
            edge = left if x == 0 else right
            lines = [lines[y] + edge[:, 128 * y : 128 * y + 128] for y in range(8)]
        scale = 1.0 / kappa[x]

        def store(q, tile):
            new[q, x] = old[q, x] - tile * scale

        from_lines(x, lambda y: lines[y], store)
        copies.append(pltpu.make_async_copy(new.at[:, x], out.at[:, x], sem.at[x]))
        copies[-1].start()
    for copy in copies:
        copy.wait()


def pack_kernel(inverse_hbm, places_hbm, out, stage, inverse, places, sem):
    copies = [pltpu.make_async_copy(inverse_hbm, inverse, sem.at[0]), pltpu.make_async_copy(places_hbm, places, sem.at[1])]
    for copy in copies:
        copy.start()
    for copy in copies:
        copy.wait()
    table = inverse[...].astype(BF16)
    numbers = iota((2048, 256), 0)
    for r in range(8):
        wanted = jnp.concatenate([places[r : r + 1, :], places[r + 8 : r + 9, :]], axis=1)
        chosen = dot(table, onehot(numbers == wanted))
        both = jnp.concatenate([chosen[:, :128], chosen[:, 128:]], axis=0)
        stage[pl.ds(r, 128, stride=8), :] = jnp.transpose(both)
    out[...] = stage[...].reshape(128, 8, 128).astype(BF16)


def unpack_kernel(arrived, inverse, slots, total, out):
    turned = jnp.transpose(arrived[...].astype(F32).reshape(1024, 128))
    table = jnp.concatenate([turned[:64], turned[64:]], axis=1).astype(BF16)
    numbers = iota((2048, 256), 0)
    for x in range(8):
        slot = slots[x]
        far = dot(table, onehot(numbers == slot))
        column = slice(256 * x, 256 * x + 256)
        weight = jnp.concatenate([total[2 * x], total[2 * x + 1]], axis=1)
        out[:, column] = jnp.where(slot < 0, inverse[:, column], far) / weight


VMEM_SPEC = pl.BlockSpec(memory_space=pltpu.VMEM)
HBM_SPEC = pl.BlockSpec(memory_space=pl.ANY)


def run(body, ins, outs, scratch=(), in_hbm=(), out_hbm=(), anywhere=(), aliases=None):
    ins = [pltpu.with_memory_space_constraint(x, pltpu.HBM) if i in in_hbm else x for i, x in enumerate(ins)]
    outs = [pltpu.HBM(x.shape, x.dtype) if i in out_hbm else x for i, x in enumerate(outs)]
    return pl.pallas_call(
        body,
        out_shape=outs,
        in_specs=[HBM_SPEC if i in in_hbm or i in anywhere else VMEM_SPEC for i in range(len(ins))],
        out_specs=[HBM_SPEC if i in out_hbm else VMEM_SPEC for i in range(len(outs))],
        scratch_shapes=list(scratch),
        input_output_aliases=aliases or {},
        compiler_params=pltpu.CompilerParams(vmem_limit_bytes=LIMIT),
    )(*ins)


def array(shape, dtype):
    return jax.ShapeDtypeStruct(shape, dtype)


def per_device(
    u_init, rhs, kappa, block_diagonal, face_coupling, smoother, restriction, coarse_inverse, segment_id, owner_device, arrival_place
):
    faces_shape = [array((16, 1024), BF16)] * 4
    state = [array((8, 64, 1024), F32), array((8, 64, 1024), BF16)]
    inverse = coarse_inverse.reshape(64, 2048)
    places = jnp.transpose(arrival_place[0])
    coupling_t = jnp.transpose(face_coupling, (0, 2, 1))

    (packed,) = run(
        pack_kernel,
        (inverse, places),
        [array((128, 8, 128), BF16)],
        [
            pltpu.VMEM((1024, 128), F32),
            pltpu.VMEM((64, 2048), F32),
            pltpu.VMEM((16, 128), I32),
            pltpu.SemaphoreType.DMA((2,)),
        ],
        in_hbm=(0, 1),
    )
    arrived = lax.all_to_all(packed, ("gx", "gy"), split_axis=0, concat_axis=0, tiled=True)
    lines = array((8, 64, 1024), BF16)
    lines_scratch = pltpu.VMEM((8, 64, 1024), BF16)
    u_p, rhs_p, *sends = run(
        start_kernel,
        (u_init, rhs, kappa, packed),
        [lines, lines] + faces_shape,
        [pltpu.VMEM((64, 8, 8, 128), BF16)] * 2
        + [pltpu.VMEM((8, 8, 128), F32)]
        + [pltpu.VMEM((8, 64, 1024), BF16)] * 2
        + [pltpu.VMEM((16, 1024), BF16)] * 4
        + [pltpu.SemaphoreType.DMA((3,)), pltpu.SemaphoreType.DMA((2, 8)), pltpu.SemaphoreType.DMA((4,))],
        in_hbm=(0, 1, 2, 3),
        out_hbm=range(6),
    )
    received = exchange(sends)
    matrix, rest, faces, rest_faces, senders, back, w, wb, c, cr = run(
        first_inner_kernel,
        (u_p, rhs_p, kappa, arrived, block_diagonal, coupling_t, smoother, restriction),
        [
            array((128, 256), BF16),
            array((16, 256), BF16),
            array((2, 256, 32), BF16),
            array((2, 32, 32), BF16),
            array((2, 32, 128), BF16),
            array((64, 16), BF16),
        ]
        + state
        + [array((8, 64, 1024), F32), array((8, 8, 1024), F32)],
        [pltpu.VMEM((80, 64), BF16)]
        + [lines_scratch] * 3
        + [pltpu.VMEM((8, 8, 128), F32), pltpu.SemaphoreType.DMA((2, 8)), pltpu.SemaphoreType.DMA],
        in_hbm=(0, 1, 2),
        anywhere=(3,),
    )
    members, members_t, total, slots = run(
        members_kernel,
        (segment_id, kappa, owner_device),
        [array((16, 128, 128), BF16)] * 2 + [array((16, 1, 128), F32), array((8, 1, 256), I32)],
    )
    (blocks,) = run(unpack_kernel, (arrived, inverse, slots, total), [array((64, 2048), F32)])

    def sides(w, wb, received, after):
        w, wb, *sends = run(
            sides_kernel,
            (w, wb, faces, senders, after, *received),
            state + faces_shape,
            anywhere=(4,),
            aliases={0: 0, 1: 1},
        )
        return w, wb, exchange(sends)

    w, wb, *sends = run(
        first_sides_kernel,
        (w, wb, faces, senders, *received),
        state + faces_shape,
        [pltpu.VMEM((16, 1024), BF16)] * 4 + [pltpu.SemaphoreType.DMA((4,))],
        anywhere=(4, 5, 6, 7),
        aliases={0: 0, 1: 1},
    )
    received = exchange(sends)
    for after in (members, blocks):
        w, wb = run(inner_kernel, (w, wb, c, matrix), state)
        w, wb, received = sides(w, wb, received, after)
    (restricted,) = run(rest_kernel, (wb, cr, rest), [array((8, 8, 1024), F32)])
    fix, *sends = run(
        coarse_kernel,
        (w, restricted, kappa, members, members_t, blocks, rest_faces, senders, back, *received),
        [array((8, 2048), F32)] + faces_shape,
        [pltpu.VMEM((8, 2048), F32)],
    )
    received = exchange(sends)
    w, wb = run(corrected_inner_kernel, (w, fix, kappa, members, back, c, matrix), state, [lines_scratch])
    w, wb, received = sides(w, wb, received, members)
    w, wb = run(inner_kernel, (w, wb, c, matrix), state)
    w, wb, received = sides(w, wb, received, members)
    (out,) = run(last_inner_kernel, (w, wb, c, matrix, kappa), [array((64, 8, 8, 128), F32)])
    (out,) = run(
        last_sides_kernel,
        (out, faces, kappa, *received),
        [array((64, 8, 8, 128), F32)],
        [pltpu.VMEM((64, 8, 8, 128), F32), pltpu.SemaphoreType.DMA((8,))],
        out_hbm=(0,),
    )
    return out


def solution(mesh):
    return jax.shard_map(
        per_device,
        mesh=mesh,
        in_specs=(
            P(None, "gx", "gy", None),
            P(None, "gx", "gy", None),
            P("gx", "gy", None),
            P(),
            P(),
            P(),
            P(),
            P(None, None, ("gx", "gy")),
            P("gx", "gy", None),
            P("gx", "gy", None),
            P(("gx", "gy"), None, None),
        ),
        out_specs=P(None, "gx", "gy", None),
        check_vma=False,
    )
```

```python
import jax
import jax.numpy as jnp
from jax import lax
from jax.experimental import pallas as pl
from jax.experimental.pallas import tpu as pltpu
from jax.sharding import PartitionSpec as P


F32 = jnp.float32
BF16 = jnp.bfloat16
I32 = jnp.int32
LIMIT = 30 * 1024 * 1024


def iota(shape, dim):
    return lax.broadcasted_iota(I32, shape, dim)


def onehot(mask):
    return jnp.where(mask, 1.0, 0.0).astype(BF16)


def dot(a, b):
    return jnp.dot(a, b, preferred_element_type=F32)


def dot_t(a, b):
    return lax.dot_general(a, b, (((1,), (1,)), ((), ())), preferred_element_type=F32)


def face_row(face, kind):
    first, second = face >> 2, face & 3
    if kind == "xl":
        return 16 * second + first
    if kind == "xh":
        return 16 * second + first + 12
    if kind == "yl":
        return 16 * second + 4 * first
    return 16 * second + 4 * first + 3


def picker(kind):
    return onehot(iota((16, 64), 1) == face_row(iota((16, 64), 0), kind)).astype(F32)


def side_weights(axis):
    here = lax.axis_index(axis)
    count = lax.axis_size(axis)
    odd = (here & 1).astype(F32)
    even = 1.0 - odd
    low = (here > 0).astype(F32)
    high = (here < count - 1).astype(F32)
    return odd, even, low, high


def face_sender(axis, low_kind, high_kind):
    odd, even, _, _ = side_weights(axis)
    low, high = picker(low_kind), picker(high_kind)
    first = jnp.concatenate([low * odd, high * even], axis=1)
    second = jnp.concatenate([low * even, high * odd], axis=1)
    return jnp.concatenate([first, second], axis=0).astype(BF16)


def face_receiver(axis, below_matrix, above_matrix):
    odd, even, low, high = side_weights(axis)
    below = jnp.concatenate([below_matrix * (odd * low), below_matrix * (even * low)], axis=1)
    above = jnp.concatenate([above_matrix * (even * high), above_matrix * (odd * high)], axis=1)
    return jnp.concatenate([below, above], axis=0).astype(BF16)


def swap(cells, axis, offset):
    count_x, count_y = lax.axis_size("gx"), lax.axis_size("gy")
    pairs = []
    for i in range(count_x):
        for j in range(count_y):
            here, count = (i, count_x) if axis == "gx" else (j, count_y)
            if offset == 0 or 0 < here < count - 1:
                other = ((here - offset) ^ 1) + offset
                target = (other, j) if axis == "gx" else (i, other)
            else:
                target = (i, j ^ 1) if axis == "gx" else (i ^ 1, j)
            pairs.append((i * count_y + j, target[0] * count_y + target[1]))
    return lax.ppermute(cells, ("gx", "gy"), pairs)


def exchange(sends):
    xa, xb, ya, yb = sends
    return swap(xa, "gx", 0), swap(xb, "gx", 1), swap(ya, "gy", 0), swap(yb, "gy", 1)


def shifted(block, step):
    lanes = iota((16, 128), 1)
    edge = 127 if step == 127 else 0
    return jnp.where(lanes == edge, 0.0, pltpu.roll(block.astype(F32), step, 1)).astype(BF16)


def neighbours(wb, x, cells_x):
    own = wb[x]
    lanes = own.shape[1]
    nothing = jnp.zeros_like(own)
    after = wb[x + 1] if x + 1 < cells_x else nothing
    before = wb[x - 1] if x > 0 else nothing
    rows = iota((64, lanes), 0)
    along_x = jnp.where((rows & 12) == 0, after, before)
    after_y = jnp.concatenate([own[:, 128:], nothing[:, :128]], axis=1)
    before_y = jnp.concatenate([nothing[:, :128], own[:, :-128]], axis=1)
    along_y = jnp.where((rows & 3) == 0, after_y, before_y)
    blocks = [slice(b, b + 128) for b in range(0, lanes, 128)]
    z_low = jnp.concatenate([shifted(own[0:16, b], 127) for b in blocks], axis=1)
    z_high = jnp.concatenate([shifted(own[48:64, b], 1) for b in blocks], axis=1)
    return jnp.concatenate([own, along_x, along_y, z_low, z_high], axis=0)


def side_changes(faces, received, rows):
    xa, xb, ya, yb = received
    out = []
    for axis, pair in ((0, (xa, xb)), (1, (ya, yb))):
        both = dot(faces[axis], jnp.concatenate([pair[0][...], pair[1][...]], axis=0))
        out += [both[0:rows] + both[rows : 2 * rows], both[2 * rows : 3 * rows] + both[3 * rows :]]
    return out


def send_faces(x_sender, y_sender, row, end, sends):
    xa, xb, ya, yb = sends
    both = dot(x_sender, jnp.concatenate([row(0), row(7)], axis=0)).astype(BF16)
    xa[...] = both[:16]
    xb[...] = both[16:]
    low = jnp.concatenate([end(x, slice(0, 128)) for x in range(8)], axis=1)
    high = jnp.concatenate([end(x, slice(896, 1024)) for x in range(8)], axis=1)
    both = dot(y_sender, jnp.concatenate([low, high], axis=0)).astype(BF16)
    ya[...] = both[:16]
    yb[...] = both[16:]


def to_lines(tile_of, target):
    for k in range(4):
        rows = {}
        for half in range(2):
            tiles = jnp.stack([tile_of(4 * (8 * half + m) + k) for m in range(8)], axis=0)
            rows[half] = jnp.swapaxes(tiles, 0, 1)
        for y in range(8):
            target(16 * k, y, jnp.concatenate([rows[0][y], rows[1][y]], axis=0))


def start_kernel(u_hbm, kappa_hbm, packed, *rest):
    faces_out, (u, kappa, wb, xa, xb, ya, yb, in_sem, face_sem) = rest[:4], rest[4:]
    kappa_copy = pltpu.make_async_copy(kappa_hbm, kappa, in_sem.at[4])
    kappa_copy.start()
    copies = [
        pltpu.make_async_copy(u_hbm.at[:, pl.ds(2 * i, 2)], u.at[:, pl.ds(2 * i, 2)], in_sem.at[i]) for i in range(4)
    ]
    for copy in copies:
        copy.start()
    kappa_copy.wait()
    for x in range(8):
        if x % 2 == 0:
            copies[x // 2].wait()
        scale = kappa[x]

        def store(p, y, value):
            if x in (0, 7) or y in (0, 7):
                wb[x, p : p + 16, 128 * y : 128 * y + 128] = value.astype(BF16)

        to_lines(lambda q: u[q, x].astype(F32) * scale, store)
    send_faces(
        face_sender("gx", "xl", "xh"),
        face_sender("gy", "yl", "yh"),
        lambda x: wb[x],
        lambda x, lanes: wb[x, :, lanes],
        (xa, xb, ya, yb),
    )
    face_copies = [
        pltpu.make_async_copy(source, target, face_sem.at[i])
        for i, (source, target) in enumerate(zip((xa, xb, ya, yb), faces_out))
    ]
    for copy in face_copies:
        copy.start()
    for copy in face_copies:
        copy.wait()


def split(full):
    high = full.astype(BF16).astype(F32)
    return jnp.concatenate([high, full - high], axis=0).astype(BF16)


def make_matrices(diag, coupling_t, smoother, restriction, matrix, rest, source, faces, rest_faces, senders, back):
    order = onehot(iota((64, 64), 1) == 4 * (iota((64, 64), 0) & 15) + (iota((64, 64), 0) >> 4))
    order_t = onehot(iota((64, 64), 0) == 4 * (iota((64, 64), 1) & 15) + (iota((64, 64), 1) >> 4))
    coupling = [jnp.transpose(coupling_t[side].astype(F32)).astype(BF16) for side in range(6)]

    def place(rows, wanted):
        column = iota((rows, 256), 1)
        p = column & 63
        face, k, i, j = iota((rows, 256), 0), p >> 4, (p >> 2) & 3, p & 3
        return onehot(wanted(column >> 6, p, face, k, i, j))

    operator = dot(diag[...], place(64, lambda part, p, f, k, i, j: (part == 0) & (f == 4 * (p & 15) + k)))
    wanted = (
        lambda part, p, f, k, i, j: (part == 1) & (i == 0) & (f == 4 * j + k),
        lambda part, p, f, k, i, j: (part == 1) & (i == 3) & (f == 4 * j + k),
        lambda part, p, f, k, i, j: (part == 2) & (j == 0) & (f == 4 * i + k),
        lambda part, p, f, k, i, j: (part == 2) & (j == 3) & (f == 4 * i + k),
        lambda part, p, f, k, i, j: (part == 3) & (p == f),
        lambda part, p, f, k, i, j: (part == 3) & (p == f + 16),
    )
    for side in range(6):
        operator = operator + dot(coupling[side], place(16, wanted[side]))
    operator = operator.astype(BF16)
    ordered = dot(order, smoother[...]).astype(BF16)
    matrix[...] = split(dot(ordered, operator))
    rest[...] = split(dot(restriction[...], operator))
    source[...] = jnp.concatenate(
        [dot(ordered, order_t), dot(restriction[...], order_t), jnp.zeros((8, 64), F32)], axis=0
    ).astype(BF16)
    one = [split(dot(ordered, coupling[side])).astype(F32) for side in range(4)]
    faces[0] = face_receiver("gx", one[1], one[0])
    faces[1] = face_receiver("gy", one[3], one[2])
    one = [split(dot(restriction[...], coupling[side])).astype(F32) for side in range(4)]
    rest_faces[0] = face_receiver("gx", one[1], one[0])
    rest_faces[1] = face_receiver("gy", one[3], one[2])
    senders[0] = face_sender("gx", "xl", "xh")
    senders[1] = face_sender("gy", "yl", "yh")
    twice = jnp.concatenate([restriction[...].astype(F32)] * 2, axis=0).astype(BF16)
    back[...] = dot_t(order, twice).astype(BF16)


def change_of(matrix, wb, x, rows):
    both = dot(matrix[:, :224], neighbours(wb, x, 8))
    return both[:rows] + both[rows:]


def first_inner_kernel(
    u_hbm, rhs_hbm, kappa_hbm, arrived, diag, coupling_t, smoother, restriction, *rest_refs
):
    outs, (w_new, wb_new, c, cr), scratch = rest_refs[:6], rest_refs[6:10], rest_refs[10:]
    source_matrix, u, rhs, wb, kappa, sem, kappa_sem = scratch
    matrix, rest, faces, rest_faces, senders, back = outs
    copies = [
        [
            pltpu.make_async_copy(source.at[:, pl.ds(2 * i, 2)], target.at[:, pl.ds(2 * i, 2)], sem.at[n, i])
            for n, (source, target) in enumerate(((u_hbm, u), (rhs_hbm, rhs)))
        ]
        for i in range(4)
    ]
    kappa_copy = pltpu.make_async_copy(kappa_hbm, kappa, kappa_sem)
    kappa_copy.start()
    for pair in copies:
        pair[0].start()
        pair[1].start()
    make_matrices(diag, coupling_t, smoother, restriction, matrix, rest, source_matrix, faces, rest_faces, senders, back)
    kappa_copy.wait()

    def scaled(x):
        if x % 2 == 0:
            copies[x // 2][0].wait()
        scale = kappa[x]

        def store(p, y, value):
            w_new[x, p : p + 16, 128 * y : 128 * y + 128] = value
            wb[x, p : p + 16, 128 * y : 128 * y + 128] = value.astype(BF16)

        to_lines(lambda q: u[q, x].astype(F32) * scale, store)

    scaled(0)
    for x in range(8):
        if x < 7:
            scaled(x + 1)
        if x % 2 == 0:
            copies[x // 2][1].wait()
        parts = {}

        def keep(p, y, value):
            parts[p, y] = value.astype(BF16)

        to_lines(lambda q: rhs[q, x].astype(F32), keep)
        lines = jnp.concatenate(
            [jnp.concatenate([parts[p, y] for y in range(8)], axis=1) for p in range(0, 64, 16)], axis=0
        )
        source = dot(source_matrix[...], lines)
        c[x] = source[0:64]
        cr[x] = source[64:72]
        new = w_new[x] + source[0:64] - change_of(matrix, wb, x, 64)
        w_new[x] = new
        wb_new[x] = new.astype(BF16)


def inner_kernel(w, wb, c, matrix, w_new, wb_new):
    for x in range(8):
        new = w[x] + c[x] - change_of(matrix, wb, x, 64)
        w_new[x] = new
        wb_new[x] = new.astype(BF16)


def add_sides(w_in, w, wb, faces, senders, received, sends):
    left, right, down, up = side_changes(faces, received, 64)
    for x in range(8):
        here = slice(x * 128, (x + 1) * 128)
        if x in (0, 7):
            edge = left if x == 0 else right
            first = edge[:, :128] + down[:, here]
            final = edge[:, -128:] + up[:, here]
            new = w_in[x] - jnp.concatenate([first, edge[:, 128:-128], final], axis=1)
            w[x] = new
            wb[x] = new.astype(BF16)
        else:
            for lanes, change in ((slice(0, 128), down), (slice(896, 1024), up)):
                new = w_in[x, :, lanes] - change[:, here]
                w[x, :, lanes] = new
                wb[x, :, lanes] = new.astype(BF16)
    send_faces(senders[0], senders[1], lambda x: wb[x], lambda x, lanes: wb[x, :, lanes], sends)


def sides_kernel(w_in, wb_in, faces, senders, after, xa, xb, ya, yb, w, wb, oxa, oxb, oya, oyb):
    add_sides(w_in, w, wb, faces, senders, (xa, xb, ya, yb), (oxa, oxb, oya, oyb))


def first_sides_kernel(w_in, wb_in, faces, senders, xa, xb, ya, yb, w, wb, oxa, oxb, oya, oyb, vxa, vxb, vya, vyb, sem):
    inside = (vxa, vxb, vya, vyb)
    copies = [pltpu.make_async_copy(s, t, sem.at[i]) for i, (s, t) in enumerate(zip((xa, xb, ya, yb), inside))]
    for copy in copies:
        copy.start()
    for copy in copies:
        copy.wait()
    add_sides(w_in, w, wb, faces, senders, inside, (oxa, oxb, oya, oyb))


def rest_kernel(wb, cr, rest, out):
    for x in range(8):
        out[x] = cr[x] - change_of(rest, wb, x, 8)


def line_mask(rows):
    return [(iota((rows, 128), 1) >> 5) == line for line in range(4)]


def members_kernel(segment, kappa, owner, members, members_t, total, slots):
    mask = line_mask(8)
    numbers = iota((32, 128), 0)
    spare = iota((8, 128), 0)
    for x in range(8):
        for half in range(2):
            group = 2 * x + half
            lines = range(4 * half, 4 * half + 4)
            hits = jnp.concatenate([onehot(numbers == segment[x, y : y + 1, :]) for y in lines], axis=0)
            members[group] = hits
            members_t[group] = jnp.transpose(hits.astype(F32)).astype(BF16)
            terms = []
            for y in lines:
                weight = kappa[x, y : y + 1, :]
                one = weight.astype(BF16).astype(F32)
                two = (weight - one).astype(BF16).astype(F32)
                last = weight - one - two
                terms.append(jnp.where(spare == 0, one, jnp.where(spare == 1, two, jnp.where(spare == 2, last, 0.0))))
            sums = dot_t(jnp.concatenate(terms, axis=0).astype(BF16), hits)
            kept = sum(jnp.where(mask[i], sums[8 * i : 8 * i + 8], 0.0) for i in range(4))
            total[group] = jnp.sum(kept, axis=0, keepdims=True)
    here = lax.axis_index(("gx", "gy"))
    earlier = onehot(iota((256, 256), 0) < iota((256, 256), 1))
    repeat = onehot(iota((32, 256), 0) == (iota((32, 256), 1) & 31))
    of_line = iota((8, 256), 0) == (iota((8, 256), 1) >> 5)
    carry = jnp.zeros((128, 1), F32)
    for x in range(8):
        repeated = dot(owner[x].astype(F32).astype(BF16), repeat)
        device = jnp.sum(jnp.where(of_line, repeated, 0.0), axis=0, keepdims=True).astype(I32)
        hits = onehot(iota((128, 256), 0) == device)
        before = dot(hits, earlier) + carry
        hits = hits.astype(F32)
        rank = jnp.sum(hits * before, axis=0, keepdims=True).astype(I32)
        carry = carry + jnp.sum(hits, axis=1, keepdims=True)
        rank = jnp.minimum(rank, 15)
        slot = (rank >> 3) * 1024 + device * 8 + (rank & 7)
        slots[x] = jnp.where(device == here, -1, slot)


def coarse_kernel(
    w, restricted, kappa, members, members_t, blocks, rest_faces, senders, back, xa, xb, ya, yb, fix_out, oxa, oxb, oya, oyb, coarse
):
    left, right, down, up = side_changes(rest_faces, (xa, xb, ya, yb), 8)
    mask = line_mask(8)
    for x in range(8):
        here = slice(x * 128, (x + 1) * 128)
        first, middle, final = down[:, here], jnp.zeros((8, 768), F32), up[:, here]
        if x in (0, 7):
            edge = left if x == 0 else right
            first, middle, final = first + edge[:, :128], edge[:, 128:-128], final + edge[:, -128:]
        fine = restricted[x] - jnp.concatenate([first, middle, final], axis=1)
        high = fine.astype(BF16).astype(F32)
        low = fine - high
        for half in range(2):
            group = 2 * x + half
            lanes = [slice(128 * y, 128 * y + 128) for y in range(4 * half, 4 * half + 4)]
            stack = jnp.concatenate([part[:, lane] for lane in lanes for part in (high, low)], axis=0)
            sums = dot(stack.astype(BF16), members_t[group])
            known = sum(
                jnp.where(mask[i], sums[16 * i : 16 * i + 8] + sums[16 * i + 8 : 16 * i + 16], 0.0) for i in range(4)
            )
            coarse[:, 128 * group : 128 * group + 128] = known
    known = coarse[...]
    fix = jnp.concatenate(
        [jnp.sum(blocks[8 * p : 8 * p + 8, :] * known, axis=0, keepdims=True) for p in range(8)], axis=0
    )
    fix_out[...] = fix
    high = fix.astype(BF16).astype(F32)
    low = fix - high

    def spread_lines(x, wanted):
        out = {}
        for half in range(2):
            group = 2 * x + half
            lanes = slice(128 * group, 128 * group + 128)
            lines = [i for i in range(4) if 4 * half + i in wanted]
            stack = jnp.concatenate(
                [jnp.where(mask[i], part[:, lanes], 0.0) for i in lines for part in (high, low)], axis=0
            )
            spread = dot(stack.astype(BF16), members[group]).astype(BF16)
            for n, i in enumerate(lines):
                out[4 * half + i] = spread[16 * n : 16 * n + 16]
        return out

    def corrected(lines):
        spread = jnp.concatenate([spreads[x][y] for x, y in lines], axis=1)
        weight = jnp.concatenate([kappa[x, y : y + 1, :] for x, y in lines], axis=1)
        old = jnp.concatenate([w[x, :, 128 * y : 128 * y + 128] for x, y in lines], axis=1)
        return (old + dot(back[...], spread) * weight).astype(BF16)

    spreads = [spread_lines(x, range(8) if x in (0, 7) else (0, 7)) for x in range(8)]
    rows = {x: corrected([(x, y) for y in range(8)]) for x in (0, 7)}
    ends = {y: corrected([(x, y) for x in range(1, 7)]) for y in (0, 7)}

    def end(x, lanes):
        if x in rows:
            return rows[x][:, lanes]
        return ends[lanes.start // 128][:, 128 * (x - 1) : 128 * x]

    send_faces(senders[0], senders[1], lambda x: rows[x], end, (oxa, oxb, oya, oyb))


def corrected_inner_kernel(w, fix, kappa, members, back, c, matrix, w_new, wb_new, wb):
    mask = line_mask(8)
    high = fix[...].astype(BF16).astype(F32)
    low = fix[...] - high
    for x in range(8):
        for half in range(2):
            group = 2 * x + half
            here = slice(512 * half, 512 * half + 512)
            lanes = slice(128 * group, 128 * group + 128)
            stack = jnp.concatenate(
                [jnp.where(mask[i], part[:, lanes], 0.0) for i in range(4) for part in (high, low)], axis=0
            )
            spread = dot(stack.astype(BF16), members[group]).astype(BF16)
            spread = jnp.concatenate([spread[16 * i : 16 * i + 16] for i in range(4)], axis=1)
            weight = jnp.concatenate([kappa[x, y : y + 1, :] for y in range(4 * half, 4 * half + 4)], axis=1)
            new = w[x, :, here] + dot(back[...], spread) * weight
            w_new[x, :, here] = new
            wb[x, :, here] = new.astype(BF16)
    for x in range(8):
        new = w_new[x] + c[x] - change_of(matrix, wb, x, 64)
        w_new[x] = new
        wb_new[x] = new.astype(BF16)


def from_lines(x, line, store):
    for k in range(4):
        for half in range(2):
            rows = slice(16 * k + 8 * half, 16 * k + 8 * half + 8)
            tiles = jnp.swapaxes(jnp.stack([line(y)[rows] for y in range(8)], axis=0), 0, 1)
            for m in range(8):
                store(4 * (8 * half + m) + k, tiles[m])


def last_inner_kernel(w, wb, c, matrix, kappa, out):
    for x in range(8):
        new = w[x] + c[x] - change_of(matrix, wb, x, 64)
        scale = 1.0 / kappa[x]

        def store(q, tile):
            out[q, x] = tile * scale

        from_lines(x, lambda y: new[:, 128 * y : 128 * y + 128], store)


def last_sides_kernel(old, faces, kappa, xa, xb, ya, yb, out, new, sem):
    left, right, down, up = side_changes(faces, (xa, xb, ya, yb), 64)
    zero = jnp.zeros((64, 128), F32)
    copies = []
    for x in range(8):
        here = slice(x * 128, (x + 1) * 128)
        lines = [down[:, here]] + [zero] * 6 + [up[:, here]]
        if x in (0, 7):
            edge = left if x == 0 else right
            lines = [lines[y] + edge[:, 128 * y : 128 * y + 128] for y in range(8)]
        scale = 1.0 / kappa[x]

        def store(q, tile):
            new[q, x] = old[q, x] - tile * scale

        from_lines(x, lambda y: lines[y], store)
        copies.append(pltpu.make_async_copy(new.at[:, x], out.at[:, x], sem.at[x]))
        copies[-1].start()
    for copy in copies:
        copy.wait()


def pack_kernel(inverse_hbm, places_hbm, out, stage, inverse, places, sem):
    copies = [pltpu.make_async_copy(inverse_hbm, inverse, sem.at[0]), pltpu.make_async_copy(places_hbm, places, sem.at[1])]
    for copy in copies:
        copy.start()
    for copy in copies:
        copy.wait()
    table = jnp.concatenate([inverse[:, 128 * n : 128 * n + 128].astype(BF16) for n in range(16)], axis=0)
    numbers = iota((128, 256), 0)
    for r in range(8):
        wanted = jnp.concatenate([places[r : r + 1, :], places[r + 8 : r + 9, :]], axis=1)
        parts = dot(table, onehot(numbers == (wanted & 127)))
        part = wanted >> 7
        chosen = sum(jnp.where(part == n, parts[64 * n : 64 * n + 64], 0.0) for n in range(16))
        both = jnp.concatenate([chosen[:, :128], chosen[:, 128:]], axis=0)
        stage[pl.ds(r, 128, stride=8), :] = jnp.transpose(both)
    out[...] = stage[...].reshape(128, 8, 128).astype(BF16)


def unpack_kernel(arrived, inverse, slots, total, out):
    turned = jnp.transpose(arrived[...].astype(F32).reshape(1024, 128))
    table = jnp.concatenate([turned[:64], turned[64:]], axis=1).astype(BF16)
    numbers = iota((2048, 256), 0)
    for x in range(8):
        slot = slots[x]
        far = dot(table, onehot(numbers == slot))
        column = slice(256 * x, 256 * x + 256)
        weight = jnp.concatenate([total[2 * x], total[2 * x + 1]], axis=1)
        out[:, column] = jnp.where(slot < 0, inverse[:, column], far) / weight


VMEM_SPEC = pl.BlockSpec(memory_space=pltpu.VMEM)
HBM_SPEC = pl.BlockSpec(memory_space=pl.ANY)


def run(body, ins, outs, scratch=(), in_hbm=(), out_hbm=(), anywhere=(), aliases=None):
    ins = [pltpu.with_memory_space_constraint(x, pltpu.HBM) if i in in_hbm else x for i, x in enumerate(ins)]
    outs = [pltpu.HBM(x.shape, x.dtype) if i in out_hbm else x for i, x in enumerate(outs)]
    return pl.pallas_call(
        body,
        out_shape=outs,
        in_specs=[HBM_SPEC if i in in_hbm or i in anywhere else VMEM_SPEC for i in range(len(ins))],
        out_specs=[HBM_SPEC if i in out_hbm else VMEM_SPEC for i in range(len(outs))],
        scratch_shapes=list(scratch),
        input_output_aliases=aliases or {},
        compiler_params=pltpu.CompilerParams(vmem_limit_bytes=LIMIT),
    )(*ins)


def array(shape, dtype):
    return jax.ShapeDtypeStruct(shape, dtype)


def per_device(
    u_init, rhs, kappa, block_diagonal, face_coupling, smoother, restriction, coarse_inverse, segment_id, owner_device, arrival_place
):
    faces_shape = [array((16, 1024), BF16)] * 4
    state = [array((8, 64, 1024), F32), array((8, 64, 1024), BF16)]
    inverse = coarse_inverse.reshape(64, 2048)
    places = jnp.transpose(arrival_place[0])
    coupling_t = jnp.transpose(face_coupling, (0, 2, 1))

    (packed,) = run(
        pack_kernel,
        (inverse, places),
        [array((128, 8, 128), BF16)],
        [
            pltpu.VMEM((1024, 128), F32),
            pltpu.VMEM((64, 2048), F32),
            pltpu.VMEM((16, 128), I32),
            pltpu.SemaphoreType.DMA((2,)),
        ],
        in_hbm=(0, 1),
    )
    arrived = lax.all_to_all(packed, ("gx", "gy"), split_axis=0, concat_axis=0, tiled=True)
    natural_scratch = pltpu.VMEM((64, 8, 8, 128), BF16)
    lines_scratch = pltpu.VMEM((8, 64, 1024), BF16)
    sends = run(
        start_kernel,
        (u_init, kappa, packed),
        faces_shape,
        [natural_scratch, pltpu.VMEM((8, 8, 128), F32), lines_scratch]
        + [pltpu.VMEM((16, 1024), BF16)] * 4
        + [pltpu.SemaphoreType.DMA((5,)), pltpu.SemaphoreType.DMA((4,))],
        in_hbm=(0, 1, 2),
        out_hbm=range(4),
    )
    received = exchange(sends)
    matrix, rest, faces, rest_faces, senders, back, w, wb, c, cr = run(
        first_inner_kernel,
        (u_init, rhs, kappa, arrived, block_diagonal, coupling_t, smoother, restriction),
        [
            array((128, 256), BF16),
            array((16, 256), BF16),
            array((2, 256, 32), BF16),
            array((2, 32, 32), BF16),
            array((2, 32, 128), BF16),
            array((64, 16), BF16),
        ]
        + state
        + [array((8, 64, 1024), F32), array((8, 8, 1024), F32)],
        [pltpu.VMEM((80, 64), BF16)]
        + [natural_scratch] * 2
        + [lines_scratch, pltpu.VMEM((8, 8, 128), F32), pltpu.SemaphoreType.DMA((2, 4)), pltpu.SemaphoreType.DMA],
        in_hbm=(0, 1, 2),
        anywhere=(3,),
    )
    members, members_t, total, slots = run(
        members_kernel,
        (segment_id, kappa, owner_device),
        [array((16, 128, 128), BF16)] * 2 + [array((16, 1, 128), F32), array((8, 1, 256), I32)],
    )
    (blocks,) = run(unpack_kernel, (arrived, inverse, slots, total), [array((64, 2048), F32)])

    def sides(w, wb, received, after):
        w, wb, *sends = run(
            sides_kernel,
            (w, wb, faces, senders, after, *received),
            state + faces_shape,
            anywhere=(4,),
            aliases={0: 0, 1: 1},
        )
        return w, wb, exchange(sends)

    w, wb, *sends = run(
        first_sides_kernel,
        (w, wb, faces, senders, *received),
        state + faces_shape,
        [pltpu.VMEM((16, 1024), BF16)] * 4 + [pltpu.SemaphoreType.DMA((4,))],
        anywhere=(4, 5, 6, 7),
        aliases={0: 0, 1: 1},
    )
    received = exchange(sends)
    for after in (members, blocks):
        w, wb = run(inner_kernel, (w, wb, c, matrix), state)
        w, wb, received = sides(w, wb, received, after)
    (restricted,) = run(rest_kernel, (wb, cr, rest), [array((8, 8, 1024), F32)])
    fix, *sends = run(
        coarse_kernel,
        (w, restricted, kappa, members, members_t, blocks, rest_faces, senders, back, *received),
        [array((8, 2048), F32)] + faces_shape,
        [pltpu.VMEM((8, 2048), F32)],
    )
    received = exchange(sends)
    w, wb = run(corrected_inner_kernel, (w, fix, kappa, members, back, c, matrix), state, [lines_scratch])
    w, wb, received = sides(w, wb, received, members)
    w, wb = run(inner_kernel, (w, wb, c, matrix), state)
    w, wb, received = sides(w, wb, received, members)
    (out,) = run(last_inner_kernel, (w, wb, c, matrix, kappa), [array((64, 8, 8, 128), F32)])
    (out,) = run(
        last_sides_kernel,
        (out, faces, kappa, *received),
        [array((64, 8, 8, 128), F32)],
        [pltpu.VMEM((64, 8, 8, 128), F32), pltpu.SemaphoreType.DMA((8,))],
        out_hbm=(0,),
    )
    return out


def solution(mesh):
    return jax.shard_map(
        per_device,
        mesh=mesh,
        in_specs=(
            P(None, "gx", "gy", None),
            P(None, "gx", "gy", None),
            P("gx", "gy", None),
            P(),
            P(),
            P(),
            P(),
            P(None, None, ("gx", "gy")),
            P("gx", "gy", None),
            P("gx", "gy", None),
            P(("gx", "gy"), None, None),
        ),
        out_specs=P(None, "gx", "gy", None),
        check_vma=False,
    )
```

```python
import functools

import jax
import jax.numpy as jnp
from jax import lax
from jax.experimental import pallas as pl
from jax.experimental.pallas import tpu as pltpu
from jax.sharding import PartitionSpec as P


F32 = jnp.float32
BF16 = jnp.bfloat16
I32 = jnp.int32
LIMIT = 30 * 1024 * 1024


def iota(shape, dim):
    return lax.broadcasted_iota(I32, shape, dim)


def onehot(mask):
    return jnp.where(mask, 1.0, 0.0).astype(BF16)


def dot(a, b):
    return jnp.dot(a, b, preferred_element_type=F32)


def dot_t(a, b):
    return lax.dot_general(a, b, (((1,), (1,)), ((), ())), preferred_element_type=F32)


def face_row(face, kind):
    first, second = face >> 2, face & 3
    if kind == "xl":
        return 16 * second + first
    if kind == "xh":
        return 16 * second + first + 12
    if kind == "yl":
        return 16 * second + 4 * first
    return 16 * second + 4 * first + 3


def picker(kind):
    return onehot(iota((16, 64), 1) == face_row(iota((16, 64), 0), kind)).astype(F32)


def side_weights(axis):
    here = lax.axis_index(axis)
    count = lax.axis_size(axis)
    odd = (here & 1).astype(F32)
    even = 1.0 - odd
    low = (here > 0).astype(F32)
    high = (here < count - 1).astype(F32)
    return odd, even, low, high


def face_sender(axis, low_kind, high_kind):
    odd, even, _, _ = side_weights(axis)
    low, high = picker(low_kind), picker(high_kind)
    first = jnp.concatenate([low * odd, high * even], axis=1)
    second = jnp.concatenate([low * even, high * odd], axis=1)
    return jnp.concatenate([first, second], axis=0).astype(BF16)


def face_receiver(axis, below_matrix, above_matrix):
    odd, even, low, high = side_weights(axis)
    below = jnp.concatenate([below_matrix * (odd * low), below_matrix * (even * low)], axis=1)
    above = jnp.concatenate([above_matrix * (even * high), above_matrix * (odd * high)], axis=1)
    return jnp.concatenate([below, above], axis=0).astype(BF16)


def swap(cells, axis, offset):
    count_x, count_y = lax.axis_size("gx"), lax.axis_size("gy")
    pairs = []
    for i in range(count_x):
        for j in range(count_y):
            here, count = (i, count_x) if axis == "gx" else (j, count_y)
            if offset == 0 or 0 < here < count - 1:
                other = ((here - offset) ^ 1) + offset
                target = (other, j) if axis == "gx" else (i, other)
            else:
                target = (i, j ^ 1) if axis == "gx" else (i ^ 1, j)
            pairs.append((i * count_y + j, target[0] * count_y + target[1]))
    return lax.ppermute(cells, ("gx", "gy"), pairs)


def exchange(sends):
    xa, xb, ya, yb = sends
    return swap(xa, "gx", 0), swap(xb, "gx", 1), swap(ya, "gy", 0), swap(yb, "gy", 1)


def shifted(block, step):
    lanes = iota((16, 128), 1)
    edge = 127 if step == 127 else 0
    return jnp.where(lanes == edge, 0.0, pltpu.roll(block.astype(F32), step, 1)).astype(BF16)


def neighbours(wb, x, cells_x):
    own = wb[x]
    lanes = own.shape[1]
    nothing = jnp.zeros_like(own)
    after = wb[x + 1] if x + 1 < cells_x else nothing
    before = wb[x - 1] if x > 0 else nothing
    rows = iota((64, lanes), 0)
    along_x = jnp.where((rows & 12) == 0, after, before)
    after_y = jnp.concatenate([own[:, 128:], nothing[:, :128]], axis=1)
    before_y = jnp.concatenate([nothing[:, :128], own[:, :-128]], axis=1)
    along_y = jnp.where((rows & 3) == 0, after_y, before_y)
    blocks = [slice(b, b + 128) for b in range(0, lanes, 128)]
    z_low = jnp.concatenate([shifted(own[0:16, b], 127) for b in blocks], axis=1)
    z_high = jnp.concatenate([shifted(own[48:64, b], 1) for b in blocks], axis=1)
    return jnp.concatenate([own, along_x, along_y, z_low, z_high], axis=0)


def side_changes(faces, received, rows):
    xa, xb, ya, yb = received
    out = []
    for axis, pair in ((0, (xa, xb)), (1, (ya, yb))):
        both = dot(faces[axis], jnp.concatenate([pair[0][...], pair[1][...]], axis=0))
        out += [both[0:rows] + both[rows : 2 * rows], both[2 * rows : 3 * rows] + both[3 * rows :]]
    return out


def send_faces(x_sender, y_sender, row, end, sends):
    xa, xb, ya, yb = sends
    both = dot(x_sender, jnp.concatenate([row(0), row(7)], axis=0)).astype(BF16)
    xa[...] = both[:16]
    xb[...] = both[16:]
    low = jnp.concatenate([end(x, slice(0, 128)) for x in range(8)], axis=1)
    high = jnp.concatenate([end(x, slice(896, 1024)) for x in range(8)], axis=1)
    both = dot(y_sender, jnp.concatenate([low, high], axis=0)).astype(BF16)
    ya[...] = both[:16]
    yb[...] = both[16:]


def to_lines(tile_of, target):
    for k in range(4):
        rows = {}
        for half in range(2):
            tiles = jnp.stack([tile_of(4 * (8 * half + m) + k) for m in range(8)], axis=0)
            rows[half] = jnp.swapaxes(tiles, 0, 1)
        for y in range(8):
            target(16 * k, y, jnp.concatenate([rows[0][y], rows[1][y]], axis=0))


def start_kernel(u_hbm, kappa_hbm, packed, *rest):
    faces_out, (u, kappa, wb, xa, xb, ya, yb, in_sem, face_sem) = rest[:4], rest[4:]
    kappa_copy = pltpu.make_async_copy(kappa_hbm, kappa, in_sem.at[4])
    kappa_copy.start()
    copies = [
        pltpu.make_async_copy(u_hbm.at[:, pl.ds(2 * i, 2)], u.at[:, pl.ds(2 * i, 2)], in_sem.at[i]) for i in range(4)
    ]
    for copy in copies:
        copy.start()
    kappa_copy.wait()
    for x in range(8):
        if x % 2 == 0:
            copies[x // 2].wait()
        scale = kappa[x]

        def store(p, y, value):
            if x in (0, 7) or y in (0, 7):
                wb[x, p : p + 16, 128 * y : 128 * y + 128] = value.astype(BF16)

        to_lines(lambda q: u[q, x].astype(F32) * scale, store)
    send_faces(
        face_sender("gx", "xl", "xh"),
        face_sender("gy", "yl", "yh"),
        lambda x: wb[x],
        lambda x, lanes: wb[x, :, lanes],
        (xa, xb, ya, yb),
    )
    face_copies = [
        pltpu.make_async_copy(source, target, face_sem.at[i])
        for i, (source, target) in enumerate(zip((xa, xb, ya, yb), faces_out))
    ]
    for copy in face_copies:
        copy.start()
    for copy in face_copies:
        copy.wait()


def split(full):
    high = full.astype(BF16).astype(F32)
    return jnp.concatenate([high, full - high], axis=0).astype(BF16)


def make_matrices(diag, coupling_t, smoother, restriction, matrix, rest, source, faces, rest_faces, senders, back):
    order = onehot(iota((64, 64), 1) == 4 * (iota((64, 64), 0) & 15) + (iota((64, 64), 0) >> 4))
    order_t = onehot(iota((64, 64), 0) == 4 * (iota((64, 64), 1) & 15) + (iota((64, 64), 1) >> 4))
    coupling = [jnp.transpose(coupling_t[side].astype(F32)).astype(BF16) for side in range(6)]

    def place(rows, wanted):
        column = iota((rows, 256), 1)
        p = column & 63
        face, k, i, j = iota((rows, 256), 0), p >> 4, (p >> 2) & 3, p & 3
        return onehot(wanted(column >> 6, p, face, k, i, j))

    operator = dot(diag[...], place(64, lambda part, p, f, k, i, j: (part == 0) & (f == 4 * (p & 15) + k)))
    wanted = (
        lambda part, p, f, k, i, j: (part == 1) & (i == 0) & (f == 4 * j + k),
        lambda part, p, f, k, i, j: (part == 1) & (i == 3) & (f == 4 * j + k),
        lambda part, p, f, k, i, j: (part == 2) & (j == 0) & (f == 4 * i + k),
        lambda part, p, f, k, i, j: (part == 2) & (j == 3) & (f == 4 * i + k),
        lambda part, p, f, k, i, j: (part == 3) & (p == f),
        lambda part, p, f, k, i, j: (part == 3) & (p == f + 16),
    )
    for side in range(6):
        operator = operator + dot(coupling[side], place(16, wanted[side]))
    operator = operator.astype(BF16)
    ordered = dot(order, smoother[...]).astype(BF16)
    matrix[...] = split(dot(ordered, operator))
    rest[...] = split(dot(restriction[...], operator))
    source[...] = jnp.concatenate(
        [dot(ordered, order_t), dot(restriction[...], order_t), jnp.zeros((8, 64), F32)], axis=0
    ).astype(BF16)
    one = [split(dot(ordered, coupling[side])).astype(F32) for side in range(4)]
    faces[0] = face_receiver("gx", one[1], one[0])
    faces[1] = face_receiver("gy", one[3], one[2])
    one = [split(dot(restriction[...], coupling[side])).astype(F32) for side in range(4)]
    rest_faces[0] = face_receiver("gx", one[1], one[0])
    rest_faces[1] = face_receiver("gy", one[3], one[2])
    senders[0] = face_sender("gx", "xl", "xh")
    senders[1] = face_sender("gy", "yl", "yh")
    twice = jnp.concatenate([restriction[...].astype(F32)] * 2, axis=0).astype(BF16)
    back[...] = dot_t(order, twice).astype(BF16)


def change_of(matrix, wb, x, rows):
    both = dot(matrix[:, :224], neighbours(wb, x, 8))
    return both[:rows] + both[rows:]


def first_inner_kernel(
    u_hbm, rhs_hbm, kappa_hbm, arrived, diag, coupling_t, smoother, restriction, *rest_refs
):
    outs, (w_new, wb_new, c, cr), scratch = rest_refs[:6], rest_refs[6:10], rest_refs[10:]
    source_matrix, u, rhs, wb, rhs_p, kappa, sem, kappa_sem = scratch
    matrix, rest, faces, rest_faces, senders, back = outs
    copies = [
        [
            pltpu.make_async_copy(source.at[:, pl.ds(2 * i, 2)], target.at[:, pl.ds(2 * i, 2)], sem.at[n, i])
            for n, (source, target) in enumerate(((u_hbm, u), (rhs_hbm, rhs)))
        ]
        for i in range(4)
    ]
    kappa_copy = pltpu.make_async_copy(kappa_hbm, kappa, kappa_sem)
    kappa_copy.start()
    for pair in copies:
        pair[0].start()
        pair[1].start()
    make_matrices(diag, coupling_t, smoother, restriction, matrix, rest, source_matrix, faces, rest_faces, senders, back)
    kappa_copy.wait()

    def scaled(x):
        if x % 2 == 0:
            copies[x // 2][0].wait()
        scale = kappa[x]

        def store(p, y, value):
            w_new[x, p : p + 16, 128 * y : 128 * y + 128] = value
            wb[x, p : p + 16, 128 * y : 128 * y + 128] = value.astype(BF16)

        to_lines(lambda q: u[q, x].astype(F32) * scale, store)

    for x in range(8):
        scaled(x)
        if x % 2 == 0:
            copies[x // 2][1].wait()

        def keep(p, y, value):
            rhs_p[x, p : p + 16, 128 * y : 128 * y + 128] = value.astype(BF16)

        to_lines(lambda q: rhs[q, x].astype(F32), keep)
    for x in range(8):
        source = dot(source_matrix[...], rhs_p[x])
        c[x] = source[0:64]
        cr[x] = source[64:72]
        new = w_new[x] + source[0:64] - change_of(matrix, wb, x, 64)
        w_new[x] = new
        wb_new[x] = new.astype(BF16)


def inner_kernel(w, wb, c, matrix, w_new, wb_new):
    for x in range(8):
        new = w[x] + c[x] - change_of(matrix, wb, x, 64)
        w_new[x] = new
        wb_new[x] = new.astype(BF16)


def add_sides(w_in, w, wb, faces, senders, received, sends):
    left, right, down, up = side_changes(faces, received, 64)
    for x in range(8):
        here = slice(x * 128, (x + 1) * 128)
        if x in (0, 7):
            edge = left if x == 0 else right
            first = edge[:, :128] + down[:, here]
            final = edge[:, -128:] + up[:, here]
            new = w_in[x] - jnp.concatenate([first, edge[:, 128:-128], final], axis=1)
            w[x] = new
            wb[x] = new.astype(BF16)
        else:
            for lanes, change in ((slice(0, 128), down), (slice(896, 1024), up)):
                new = w_in[x, :, lanes] - change[:, here]
                w[x, :, lanes] = new
                wb[x, :, lanes] = new.astype(BF16)
    send_faces(senders[0], senders[1], lambda x: wb[x], lambda x, lanes: wb[x, :, lanes], sends)


def sides_kernel(w_in, wb_in, faces, senders, after, xa, xb, ya, yb, w, wb, oxa, oxb, oya, oyb):
    add_sides(w_in, w, wb, faces, senders, (xa, xb, ya, yb), (oxa, oxb, oya, oyb))


def first_sides_kernel(w_in, wb_in, faces, senders, xa, xb, ya, yb, w, wb, oxa, oxb, oya, oyb, vxa, vxb, vya, vyb, sem):
    inside = (vxa, vxb, vya, vyb)
    copies = [pltpu.make_async_copy(s, t, sem.at[i]) for i, (s, t) in enumerate(zip((xa, xb, ya, yb), inside))]
    for copy in copies:
        copy.start()
    for copy in copies:
        copy.wait()
    add_sides(w_in, w, wb, faces, senders, inside, (oxa, oxb, oya, oyb))


def rest_kernel(wb, cr, rest, out):
    for x in range(8):
        out[x] = cr[x] - change_of(rest, wb, x, 8)


def line_mask(rows):
    return [(iota((rows, 128), 1) >> 5) == line for line in range(4)]


def members_kernel(segment, kappa, owner, members, members_t, total, slots):
    mask = line_mask(8)
    numbers = iota((32, 128), 0)
    spare = iota((8, 128), 0)
    for x in range(8):
        for half in range(2):
            group = 2 * x + half
            lines = range(4 * half, 4 * half + 4)
            hits = jnp.concatenate([onehot(numbers == segment[x, y : y + 1, :]) for y in lines], axis=0)
            members[group] = hits
            members_t[group] = jnp.transpose(hits.astype(F32)).astype(BF16)
            terms = []
            for y in lines:
                weight = kappa[x, y : y + 1, :]
                one = weight.astype(BF16).astype(F32)
                two = (weight - one).astype(BF16).astype(F32)
                last = weight - one - two
                terms.append(jnp.where(spare == 0, one, jnp.where(spare == 1, two, jnp.where(spare == 2, last, 0.0))))
            sums = dot_t(jnp.concatenate(terms, axis=0).astype(BF16), hits)
            kept = sum(jnp.where(mask[i], sums[8 * i : 8 * i + 8], 0.0) for i in range(4))
            total[group] = jnp.sum(kept, axis=0, keepdims=True)
    here = lax.axis_index(("gx", "gy"))
    earlier = onehot(iota((256, 256), 0) < iota((256, 256), 1))
    repeat = onehot(iota((32, 256), 0) == (iota((32, 256), 1) & 31))
    of_line = iota((8, 256), 0) == (iota((8, 256), 1) >> 5)
    carry = jnp.zeros((128, 1), F32)
    for x in range(8):
        repeated = dot(owner[x].astype(F32).astype(BF16), repeat)
        device = jnp.sum(jnp.where(of_line, repeated, 0.0), axis=0, keepdims=True).astype(I32)
        hits = onehot(iota((128, 256), 0) == device)
        before = dot(hits, earlier) + carry
        hits = hits.astype(F32)
        rank = jnp.sum(hits * before, axis=0, keepdims=True).astype(I32)
        carry = carry + jnp.sum(hits, axis=1, keepdims=True)
        rank = jnp.minimum(rank, 15)
        slot = (rank >> 3) * 1024 + device * 8 + (rank & 7)
        slots[x] = jnp.where(device == here, -1, slot)


def coarse_kernel(
    w, restricted, kappa, members, members_t, first_half, second_half, rest_faces, senders, back, xa, xb, ya, yb, fix_out, oxa, oxb, oya, oyb, coarse
):
    left, right, down, up = side_changes(rest_faces, (xa, xb, ya, yb), 8)
    mask = line_mask(8)
    for x in range(8):
        here = slice(x * 128, (x + 1) * 128)
        first, middle, final = down[:, here], jnp.zeros((8, 768), F32), up[:, here]
        if x in (0, 7):
            edge = left if x == 0 else right
            first, middle, final = first + edge[:, :128], edge[:, 128:-128], final + edge[:, -128:]
        fine = restricted[x] - jnp.concatenate([first, middle, final], axis=1)
        high = fine.astype(BF16).astype(F32)
        low = fine - high
        for half in range(2):
            group = 2 * x + half
            lanes = [slice(128 * y, 128 * y + 128) for y in range(4 * half, 4 * half + 4)]
            stack = jnp.concatenate([part[:, lane] for lane in lanes for part in (high, low)], axis=0)
            sums = dot(stack.astype(BF16), members_t[group])
            known = sum(
                jnp.where(mask[i], sums[16 * i : 16 * i + 8] + sums[16 * i + 8 : 16 * i + 16], 0.0) for i in range(4)
            )
            coarse[:, 128 * group : 128 * group + 128] = known
    fix = jnp.concatenate(
        [
            jnp.concatenate(
                [
                    jnp.sum(blocks[8 * p : 8 * p + 8, :] * coarse[:, lanes], axis=0, keepdims=True)
                    for blocks, lanes in ((first_half, slice(0, 1024)), (second_half, slice(1024, 2048)))
                ],
                axis=1,
            )
            for p in range(8)
        ],
        axis=0,
    )
    fix_out[...] = fix
    high = fix.astype(BF16).astype(F32)
    low = fix - high

    def spread_lines(x, wanted):
        out = {}
        for half in range(2):
            group = 2 * x + half
            lanes = slice(128 * group, 128 * group + 128)
            lines = [i for i in range(4) if 4 * half + i in wanted]
            stack = jnp.concatenate(
                [jnp.where(mask[i], part[:, lanes], 0.0) for i in lines for part in (high, low)], axis=0
            )
            spread = dot(stack.astype(BF16), members[group]).astype(BF16)
            for n, i in enumerate(lines):
                out[4 * half + i] = spread[16 * n : 16 * n + 16]
        return out

    def corrected(lines):
        spread = jnp.concatenate([spreads[x][y] for x, y in lines], axis=1)
        weight = jnp.concatenate([kappa[x, y : y + 1, :] for x, y in lines], axis=1)
        old = jnp.concatenate([w[x, :, 128 * y : 128 * y + 128] for x, y in lines], axis=1)
        return (old + dot(back[...], spread) * weight).astype(BF16)

    spreads = [spread_lines(x, range(8) if x in (0, 7) else (0, 7)) for x in range(8)]
    rows = {x: corrected([(x, y) for y in range(8)]) for x in (0, 7)}
    ends = {y: corrected([(x, y) for x in range(1, 7)]) for y in (0, 7)}

    def end(x, lanes):
        if x in rows:
            return rows[x][:, lanes]
        return ends[lanes.start // 128][:, 128 * (x - 1) : 128 * x]

    send_faces(senders[0], senders[1], lambda x: rows[x], end, (oxa, oxb, oya, oyb))


def corrected_inner_kernel(w, fix, kappa, members, back, c, matrix, w_new, wb_new, wb, spreads):
    mask = line_mask(8)
    high = fix[...].astype(BF16).astype(F32)
    low = fix[...] - high

    for x in range(8):
        for half in range(2):
            group = 2 * x + half
            lanes = slice(128 * group, 128 * group + 128)
            stack = jnp.concatenate(
                [jnp.where(mask[i], part[:, lanes], 0.0) for i in range(4) for part in (high, low)], axis=0
            )
            spread = dot(stack.astype(BF16), members[group]).astype(BF16)
            for i in range(4):
                y = 4 * half + i
                spreads[x, :, 128 * y : 128 * y + 128] = spread[16 * i : 16 * i + 16]
    for x in range(8):
        weight = jnp.concatenate([kappa[x, y : y + 1, :] for y in range(8)], axis=1)
        new = w[x] + dot(back[...], spreads[x]) * weight
        w_new[x] = new
        wb[x] = new.astype(BF16)
    for x in range(8):
        new = w_new[x] + c[x] - change_of(matrix, wb, x, 64)
        w_new[x] = new
        wb_new[x] = new.astype(BF16)


def from_lines(x, line, store):
    for k in range(4):
        for half in range(2):
            rows = slice(16 * k + 8 * half, 16 * k + 8 * half + 8)
            tiles = jnp.swapaxes(jnp.stack([line(y)[rows] for y in range(8)], axis=0), 0, 1)
            for m in range(8):
                store(4 * (8 * half + m) + k, tiles[m])


def last_inner_kernel(w, wb, c, matrix, kappa, out):
    for x in range(8):
        new = w[x] + c[x] - change_of(matrix, wb, x, 64)
        scale = 1.0 / kappa[x]

        def store(q, tile):
            out[q, x] = tile * scale

        from_lines(x, lambda y: new[:, 128 * y : 128 * y + 128], store)


def last_sides_kernel(old, faces, kappa, xa, xb, ya, yb, out, new, sem):
    left, right, down, up = side_changes(faces, (xa, xb, ya, yb), 64)
    zero = jnp.zeros((64, 128), F32)
    copies = []
    for x in range(8):
        here = slice(x * 128, (x + 1) * 128)
        lines = [down[:, here]] + [zero] * 6 + [up[:, here]]
        if x in (0, 7):
            edge = left if x == 0 else right
            lines = [lines[y] + edge[:, 128 * y : 128 * y + 128] for y in range(8)]
        scale = 1.0 / kappa[x]

        def store(q, tile):
            new[q, x] = old[q, x] - tile * scale

        from_lines(x, lambda y: lines[y], store)
        copies.append(pltpu.make_async_copy(new.at[:, x], out.at[:, x], sem.at[x]))
        copies[-1].start()
    for copy in copies:
        copy.wait()


def pack_kernel(inverse_hbm, places_hbm, out, stage, inverse, places, sem):
    copies = [pltpu.make_async_copy(inverse_hbm, inverse, sem.at[0]), pltpu.make_async_copy(places_hbm, places, sem.at[1])]
    for copy in copies:
        copy.start()
    for copy in copies:
        copy.wait()
    table = jnp.concatenate([inverse[:, 128 * n : 128 * n + 128].astype(BF16) for n in range(16)], axis=0)
    numbers = iota((128, 256), 0)
    for r in range(8):
        wanted = jnp.concatenate([places[r : r + 1, :], places[r + 8 : r + 9, :]], axis=1)
        parts = dot(table, onehot(numbers == (wanted & 127)))
        part = wanted >> 7
        chosen = sum(jnp.where(part == n, parts[64 * n : 64 * n + 64], 0.0) for n in range(16))
        both = jnp.concatenate([chosen[:, :128], chosen[:, 128:]], axis=0)
        stage[pl.ds(r, 128, stride=8), :] = jnp.transpose(both)
    out[...] = stage[...].reshape(128, 8, 128).astype(BF16)


def unpack_kernel(start, arrived, inverse, slots, total, out):
    turned = jnp.transpose(arrived[...].astype(F32).reshape(1024, 128))
    table = jnp.concatenate([turned[:64], turned[64:]], axis=1).astype(BF16)
    numbers = iota((2048, 256), 0)
    for n in range(4):
        x = start + n
        slot = slots[x]
        far = dot(table, onehot(numbers == slot))
        weight = jnp.concatenate([total[2 * x], total[2 * x + 1]], axis=1)
        own = inverse[:, 256 * x : 256 * x + 256]
        out[:, 256 * n : 256 * n + 256] = jnp.where(slot < 0, own, far) / weight


VMEM_SPEC = pl.BlockSpec(memory_space=pltpu.VMEM)
HBM_SPEC = pl.BlockSpec(memory_space=pl.ANY)


def run(body, ins, outs, scratch=(), in_hbm=(), out_hbm=(), anywhere=(), aliases=None):
    ins = [pltpu.with_memory_space_constraint(x, pltpu.HBM) if i in in_hbm else x for i, x in enumerate(ins)]
    outs = [pltpu.HBM(x.shape, x.dtype) if i in out_hbm else x for i, x in enumerate(outs)]
    return pl.pallas_call(
        body,
        out_shape=outs,
        in_specs=[HBM_SPEC if i in in_hbm or i in anywhere else VMEM_SPEC for i in range(len(ins))],
        out_specs=[HBM_SPEC if i in out_hbm else VMEM_SPEC for i in range(len(outs))],
        scratch_shapes=list(scratch),
        input_output_aliases=aliases or {},
        compiler_params=pltpu.CompilerParams(vmem_limit_bytes=LIMIT),
    )(*ins)


def array(shape, dtype):
    return jax.ShapeDtypeStruct(shape, dtype)


def per_device(
    u_init, rhs, kappa, block_diagonal, face_coupling, smoother, restriction, coarse_inverse, segment_id, owner_device, arrival_place
):
    faces_shape = [array((16, 1024), BF16)] * 4
    state = [array((8, 64, 1024), F32), array((8, 64, 1024), BF16)]
    inverse = coarse_inverse.reshape(64, 2048)
    places = jnp.transpose(arrival_place[0])
    coupling_t = jnp.transpose(face_coupling, (0, 2, 1))

    (packed,) = run(
        pack_kernel,
        (inverse, places),
        [array((128, 8, 128), BF16)],
        [
            pltpu.VMEM((1024, 128), F32),
            pltpu.VMEM((64, 2048), F32),
            pltpu.VMEM((16, 128), I32),
            pltpu.SemaphoreType.DMA((2,)),
        ],
        in_hbm=(0, 1),
    )
    arrived = lax.all_to_all(packed, ("gx", "gy"), split_axis=0, concat_axis=0, tiled=True)
    natural_scratch = pltpu.VMEM((64, 8, 8, 128), BF16)
    lines_scratch = pltpu.VMEM((8, 64, 1024), BF16)
    sends = run(
        start_kernel,
        (u_init, kappa, packed),
        faces_shape,
        [natural_scratch, pltpu.VMEM((8, 8, 128), F32), lines_scratch]
        + [pltpu.VMEM((16, 1024), BF16)] * 4
        + [pltpu.SemaphoreType.DMA((5,)), pltpu.SemaphoreType.DMA((4,))],
        in_hbm=(0, 1, 2),
        out_hbm=range(4),
    )
    received = exchange(sends)
    matrix, rest, faces, rest_faces, senders, back, w, wb, c, cr = run(
        first_inner_kernel,
        (u_init, rhs, kappa, arrived, block_diagonal, coupling_t, smoother, restriction),
        [
            array((128, 256), BF16),
            array((16, 256), BF16),
            array((2, 256, 32), BF16),
            array((2, 32, 32), BF16),
            array((2, 32, 128), BF16),
            array((64, 16), BF16),
        ]
        + state
        + [array((8, 64, 1024), F32), array((8, 8, 1024), F32)],
        [pltpu.VMEM((80, 64), BF16)]
        + [natural_scratch] * 2
        + [lines_scratch] * 2
        + [pltpu.VMEM((8, 8, 128), F32), pltpu.SemaphoreType.DMA((2, 4)), pltpu.SemaphoreType.DMA],
        in_hbm=(0, 1, 2),
        anywhere=(3,),
    )
    members, members_t, total, slots = run(
        members_kernel,
        (segment_id, kappa, owner_device),
        [array((16, 128, 128), BF16)] * 2 + [array((16, 1, 128), F32), array((8, 1, 256), I32)],
    )
    halves = [
        run(functools.partial(unpack_kernel, start), (arrived, inverse, slots, total), [array((64, 1024), F32)])[0]
        for start in (0, 4)
    ]

    def sides(w, wb, received, after):
        w, wb, *sends = run(
            sides_kernel,
            (w, wb, faces, senders, after, *received),
            state + faces_shape,
            anywhere=(4,),
            aliases={0: 0, 1: 1},
        )
        return w, wb, exchange(sends)

    w, wb, *sends = run(
        first_sides_kernel,
        (w, wb, faces, senders, *received),
        state + faces_shape,
        [pltpu.VMEM((16, 1024), BF16)] * 4 + [pltpu.SemaphoreType.DMA((4,))],
        anywhere=(4, 5, 6, 7),
        aliases={0: 0, 1: 1},
    )
    received = exchange(sends)
    for after in (members, halves[0]):
        w, wb = run(inner_kernel, (w, wb, c, matrix), state)
        w, wb, received = sides(w, wb, received, after)
    (restricted,) = run(rest_kernel, (wb, cr, rest), [array((8, 8, 1024), F32)])
    fix, *sends = run(
        coarse_kernel,
        (w, restricted, kappa, members, members_t, *halves, rest_faces, senders, back, *received),
        [array((8, 2048), F32)] + faces_shape,
        [pltpu.VMEM((8, 2048), F32)],
    )
    received = exchange(sends)
    w, wb = run(corrected_inner_kernel, (w, fix, kappa, members, back, c, matrix), state, [lines_scratch, pltpu.VMEM((8, 16, 1024), BF16)])
    w, wb, received = sides(w, wb, received, members)
    w, wb = run(inner_kernel, (w, wb, c, matrix), state)
    w, wb, received = sides(w, wb, received, members)
    (out,) = run(last_inner_kernel, (w, wb, c, matrix, kappa), [array((64, 8, 8, 128), F32)])
    (out,) = run(
        last_sides_kernel,
        (out, faces, kappa, *received),
        [array((64, 8, 8, 128), F32)],
        [pltpu.VMEM((64, 8, 8, 128), F32), pltpu.SemaphoreType.DMA((8,))],
        out_hbm=(0,),
    )
    return out


def solution(mesh):
    return jax.shard_map(
        per_device,
        mesh=mesh,
        in_specs=(
            P(None, "gx", "gy", None),
            P(None, "gx", "gy", None),
            P("gx", "gy", None),
            P(),
            P(),
            P(),
            P(),
            P(None, None, ("gx", "gy")),
            P("gx", "gy", None),
            P("gx", "gy", None),
            P(("gx", "gy"), None, None),
        ),
        out_specs=P(None, "gx", "gy", None),
        check_vma=False,
    )
```

```python
import functools

import jax
import jax.numpy as jnp
from jax import lax
from jax.experimental import pallas as pl
from jax.experimental.pallas import tpu as pltpu
from jax.sharding import PartitionSpec as P


F32 = jnp.float32
BF16 = jnp.bfloat16
I32 = jnp.int32
LIMIT = 30 * 1024 * 1024


def iota(shape, dim):
    return lax.broadcasted_iota(I32, shape, dim)


def onehot(mask):
    return jnp.where(mask, 1.0, 0.0).astype(BF16)


def dot(a, b):
    return jnp.dot(a, b, preferred_element_type=F32)


def dot_t(a, b):
    return lax.dot_general(a, b, (((1,), (1,)), ((), ())), preferred_element_type=F32)


def face_row(face, kind):
    first, second = face >> 2, face & 3
    if kind == "xl":
        return 16 * second + first
    if kind == "xh":
        return 16 * second + first + 12
    if kind == "yl":
        return 16 * second + 4 * first
    return 16 * second + 4 * first + 3


def picker(kind):
    return onehot(iota((16, 64), 1) == face_row(iota((16, 64), 0), kind)).astype(F32)


def side_weights(axis):
    here = lax.axis_index(axis)
    count = lax.axis_size(axis)
    odd = (here & 1).astype(F32)
    even = 1.0 - odd
    low = (here > 0).astype(F32)
    high = (here < count - 1).astype(F32)
    return odd, even, low, high


def face_sender(axis, low_kind, high_kind):
    odd, even, _, _ = side_weights(axis)
    low, high = picker(low_kind), picker(high_kind)
    first = jnp.concatenate([low * odd, high * even], axis=1)
    second = jnp.concatenate([low * even, high * odd], axis=1)
    return jnp.concatenate([first, second], axis=0).astype(BF16)


def face_receiver(axis, below_matrix, above_matrix):
    odd, even, low, high = side_weights(axis)
    below = jnp.concatenate([below_matrix * (odd * low), below_matrix * (even * low)], axis=1)
    above = jnp.concatenate([above_matrix * (even * high), above_matrix * (odd * high)], axis=1)
    return jnp.concatenate([below, above], axis=0).astype(BF16)


def swap(cells, axis, offset):
    count_x, count_y = lax.axis_size("gx"), lax.axis_size("gy")
    pairs = []
    for i in range(count_x):
        for j in range(count_y):
            here, count = (i, count_x) if axis == "gx" else (j, count_y)
            if offset == 0 or 0 < here < count - 1:
                other = ((here - offset) ^ 1) + offset
                target = (other, j) if axis == "gx" else (i, other)
            else:
                target = (i, j ^ 1) if axis == "gx" else (i ^ 1, j)
            pairs.append((i * count_y + j, target[0] * count_y + target[1]))
    return lax.ppermute(cells, ("gx", "gy"), pairs)


def exchange(sends):
    xa, xb, ya, yb = sends
    return swap(xa, "gx", 0), swap(xb, "gx", 1), swap(ya, "gy", 0), swap(yb, "gy", 1)


def shifted(block, step):
    lanes = iota((16, 128), 1)
    edge = 127 if step == 127 else 0
    return jnp.where(lanes == edge, 0.0, pltpu.roll(block.astype(F32), step, 1)).astype(BF16)


def neighbours(wb, x, cells_x):
    own = wb[x]
    lanes = own.shape[1]
    nothing = jnp.zeros_like(own)
    after = wb[x + 1] if x + 1 < cells_x else nothing
    before = wb[x - 1] if x > 0 else nothing
    rows = iota((64, lanes), 0)
    along_x = jnp.where((rows & 12) == 0, after, before)
    after_y = jnp.concatenate([own[:, 128:], nothing[:, :128]], axis=1)
    before_y = jnp.concatenate([nothing[:, :128], own[:, :-128]], axis=1)
    along_y = jnp.where((rows & 3) == 0, after_y, before_y)
    blocks = [slice(b, b + 128) for b in range(0, lanes, 128)]
    z_low = jnp.concatenate([shifted(own[0:16, b], 127) for b in blocks], axis=1)
    z_high = jnp.concatenate([shifted(own[48:64, b], 1) for b in blocks], axis=1)
    return jnp.concatenate([own, along_x, along_y, z_low, z_high], axis=0)


def side_changes(faces, received, rows):
    xa, xb, ya, yb = received
    out = []
    for axis, pair in ((0, (xa, xb)), (1, (ya, yb))):
        both = dot(faces[axis], jnp.concatenate([pair[0][...], pair[1][...]], axis=0))
        out += [both[0:rows] + both[rows : 2 * rows], both[2 * rows : 3 * rows] + both[3 * rows :]]
    return out


def send_faces(x_sender, y_sender, row, end, sends):
    xa, xb, ya, yb = sends
    both = dot(x_sender, jnp.concatenate([row(0), row(7)], axis=0)).astype(BF16)
    xa[...] = both[:16]
    xb[...] = both[16:]
    low = jnp.concatenate([end(x, slice(0, 128)) for x in range(8)], axis=1)
    high = jnp.concatenate([end(x, slice(896, 1024)) for x in range(8)], axis=1)
    both = dot(y_sender, jnp.concatenate([low, high], axis=0)).astype(BF16)
    ya[...] = both[:16]
    yb[...] = both[16:]


def to_lines(tile_of, target):
    for k in range(4):
        rows = {}
        for half in range(2):
            tiles = jnp.stack([tile_of(4 * (8 * half + m) + k) for m in range(8)], axis=0)
            rows[half] = jnp.swapaxes(tiles, 0, 1)
        for y in range(8):
            target(16 * k, y, jnp.concatenate([rows[0][y], rows[1][y]], axis=0))


def start_kernel(u_hbm, kappa_hbm, packed, *rest):
    faces_out, (u, kappa, wb, xa, xb, ya, yb, in_sem, face_sem) = rest[:4], rest[4:]
    kappa_copy = pltpu.make_async_copy(kappa_hbm, kappa, in_sem.at[4])
    kappa_copy.start()
    copies = [
        pltpu.make_async_copy(u_hbm.at[:, pl.ds(2 * i, 2)], u.at[:, pl.ds(2 * i, 2)], in_sem.at[i]) for i in range(4)
    ]
    for copy in copies:
        copy.start()
    kappa_copy.wait()
    for x in range(8):
        if x % 2 == 0:
            copies[x // 2].wait()
        scale = kappa[x]

        def store(p, y, value):
            if x in (0, 7) or y in (0, 7):
                wb[x, p : p + 16, 128 * y : 128 * y + 128] = value.astype(BF16)

        to_lines(lambda q: u[q, x].astype(F32) * scale, store)
    send_faces(
        face_sender("gx", "xl", "xh"),
        face_sender("gy", "yl", "yh"),
        lambda x: wb[x],
        lambda x, lanes: wb[x, :, lanes],
        (xa, xb, ya, yb),
    )
    face_copies = [
        pltpu.make_async_copy(source, target, face_sem.at[i])
        for i, (source, target) in enumerate(zip((xa, xb, ya, yb), faces_out))
    ]
    for copy in face_copies:
        copy.start()
    for copy in face_copies:
        copy.wait()


def split(full):
    high = full.astype(BF16).astype(F32)
    return jnp.concatenate([high, full - high], axis=0).astype(BF16)


def make_matrices(diag, coupling_t, smoother, restriction, matrix, rest, source, faces, rest_faces, senders, back):
    order = onehot(iota((64, 64), 1) == 4 * (iota((64, 64), 0) & 15) + (iota((64, 64), 0) >> 4))
    order_t = onehot(iota((64, 64), 0) == 4 * (iota((64, 64), 1) & 15) + (iota((64, 64), 1) >> 4))
    coupling = [jnp.transpose(coupling_t[side].astype(F32)).astype(BF16) for side in range(6)]

    def place(rows, wanted):
        column = iota((rows, 256), 1)
        p = column & 63
        face, k, i, j = iota((rows, 256), 0), p >> 4, (p >> 2) & 3, p & 3
        return onehot(wanted(column >> 6, p, face, k, i, j))

    operator = dot(diag[...], place(64, lambda part, p, f, k, i, j: (part == 0) & (f == 4 * (p & 15) + k)))
    wanted = (
        lambda part, p, f, k, i, j: (part == 1) & (i == 0) & (f == 4 * j + k),
        lambda part, p, f, k, i, j: (part == 1) & (i == 3) & (f == 4 * j + k),
        lambda part, p, f, k, i, j: (part == 2) & (j == 0) & (f == 4 * i + k),
        lambda part, p, f, k, i, j: (part == 2) & (j == 3) & (f == 4 * i + k),
        lambda part, p, f, k, i, j: (part == 3) & (p == f),
        lambda part, p, f, k, i, j: (part == 3) & (p == f + 16),
    )
    for side in range(6):
        operator = operator + dot(coupling[side], place(16, wanted[side]))
    operator = operator.astype(BF16)
    ordered = dot(order, smoother[...]).astype(BF16)
    matrix[...] = split(dot(ordered, operator))
    rest[...] = split(dot(restriction[...], operator))
    source[...] = jnp.concatenate(
        [dot(ordered, order_t), dot(restriction[...], order_t), jnp.zeros((8, 64), F32)], axis=0
    ).astype(BF16)
    one = [split(dot(ordered, coupling[side])).astype(F32) for side in range(4)]
    faces[0] = face_receiver("gx", one[1], one[0])
    faces[1] = face_receiver("gy", one[3], one[2])
    one = [split(dot(restriction[...], coupling[side])).astype(F32) for side in range(4)]
    rest_faces[0] = face_receiver("gx", one[1], one[0])
    rest_faces[1] = face_receiver("gy", one[3], one[2])
    senders[0] = face_sender("gx", "xl", "xh")
    senders[1] = face_sender("gy", "yl", "yh")
    twice = jnp.concatenate([restriction[...].astype(F32)] * 2, axis=0).astype(BF16)
    back[...] = dot_t(order, twice).astype(BF16)


def change_of(matrix, wb, x, rows):
    both = dot(matrix[:, :224], neighbours(wb, x, 8))
    return both[:rows] + both[rows:]


def first_inner_kernel(
    u_hbm, rhs_hbm, kappa_hbm, arrived, diag, coupling_t, smoother, restriction, *rest_refs
):
    outs, (w_new, wb_new, c, cr), scratch = rest_refs[:6], rest_refs[6:10], rest_refs[10:]
    source_matrix, u, rhs, wb, rhs_p, kappa, sem, kappa_sem = scratch
    matrix, rest, faces, rest_faces, senders, back = outs
    copies = [
        [
            pltpu.make_async_copy(source.at[:, pl.ds(2 * i, 2)], target.at[:, pl.ds(2 * i, 2)], sem.at[n, i])
            for n, (source, target) in enumerate(((u_hbm, u), (rhs_hbm, rhs)))
        ]
        for i in range(4)
    ]
    kappa_copy = pltpu.make_async_copy(kappa_hbm, kappa, kappa_sem)
    kappa_copy.start()
    for pair in copies:
        pair[0].start()
        pair[1].start()
    make_matrices(diag, coupling_t, smoother, restriction, matrix, rest, source_matrix, faces, rest_faces, senders, back)
    kappa_copy.wait()

    def scaled(x):
        if x % 2 == 0:
            copies[x // 2][0].wait()
        scale = kappa[x]

        def store(p, y, value):
            w_new[x, p : p + 16, 128 * y : 128 * y + 128] = value
            wb[x, p : p + 16, 128 * y : 128 * y + 128] = value.astype(BF16)

        to_lines(lambda q: u[q, x].astype(F32) * scale, store)

    for x in range(8):
        scaled(x)
        if x % 2 == 0:
            copies[x // 2][1].wait()

        def keep(p, y, value):
            rhs_p[x, p : p + 16, 128 * y : 128 * y + 128] = value.astype(BF16)

        to_lines(lambda q: rhs[q, x].astype(F32), keep)
    for x in range(8):
        source = dot(source_matrix[...], rhs_p[x])
        c[x] = source[0:64]
        cr[x] = source[64:72]
        new = w_new[x] + source[0:64] - change_of(matrix, wb, x, 64)
        w_new[x] = new
        wb_new[x] = new.astype(BF16)


def inner_kernel(w, wb, c, matrix, w_new, wb_new):
    for x in range(8):
        new = w[x] + c[x] - change_of(matrix, wb, x, 64)
        w_new[x] = new
        wb_new[x] = new.astype(BF16)


def add_sides(w_in, w, wb, faces, senders, received, sends):
    left, right, down, up = side_changes(faces, received, 64)
    for x in range(8):
        here = slice(x * 128, (x + 1) * 128)
        if x in (0, 7):
            edge = left if x == 0 else right
            first = edge[:, :128] + down[:, here]
            final = edge[:, -128:] + up[:, here]
            new = w_in[x] - jnp.concatenate([first, edge[:, 128:-128], final], axis=1)
            w[x] = new
            wb[x] = new.astype(BF16)
        else:
            for lanes, change in ((slice(0, 128), down), (slice(896, 1024), up)):
                new = w_in[x, :, lanes] - change[:, here]
                w[x, :, lanes] = new
                wb[x, :, lanes] = new.astype(BF16)
    send_faces(senders[0], senders[1], lambda x: wb[x], lambda x, lanes: wb[x, :, lanes], sends)


def sides_kernel(w_in, wb_in, faces, senders, after, xa, xb, ya, yb, w, wb, oxa, oxb, oya, oyb):
    add_sides(w_in, w, wb, faces, senders, (xa, xb, ya, yb), (oxa, oxb, oya, oyb))


def first_sides_kernel(w_in, wb_in, faces, senders, xa, xb, ya, yb, w, wb, oxa, oxb, oya, oyb, vxa, vxb, vya, vyb, sem):
    inside = (vxa, vxb, vya, vyb)
    copies = [pltpu.make_async_copy(s, t, sem.at[i]) for i, (s, t) in enumerate(zip((xa, xb, ya, yb), inside))]
    for copy in copies:
        copy.start()
    for copy in copies:
        copy.wait()
    add_sides(w_in, w, wb, faces, senders, inside, (oxa, oxb, oya, oyb))


def rest_kernel(wb, cr, rest, out):
    for x in range(8):
        out[x] = cr[x] - change_of(rest, wb, x, 8)


def line_mask(rows):
    return [(iota((rows, 128), 1) >> 5) == line for line in range(4)]


def members_kernel(segment, kappa, owner, members, members_t, total, slots):
    mask = line_mask(8)
    numbers = iota((32, 128), 0)
    spare = iota((8, 128), 0)
    for x in range(8):
        for half in range(2):
            group = 2 * x + half
            lines = range(4 * half, 4 * half + 4)
            hits = jnp.concatenate([onehot(numbers == segment[x, y : y + 1, :]) for y in lines], axis=0)
            members[group] = hits
            members_t[group] = jnp.transpose(hits.astype(F32)).astype(BF16)
            terms = []
            for y in lines:
                weight = kappa[x, y : y + 1, :]
                one = weight.astype(BF16).astype(F32)
                two = (weight - one).astype(BF16).astype(F32)
                last = weight - one - two
                terms.append(jnp.where(spare == 0, one, jnp.where(spare == 1, two, jnp.where(spare == 2, last, 0.0))))
            sums = dot_t(jnp.concatenate(terms, axis=0).astype(BF16), hits)
            kept = sum(jnp.where(mask[i], sums[8 * i : 8 * i + 8], 0.0) for i in range(4))
            total[group] = jnp.sum(kept, axis=0, keepdims=True)
    here = lax.axis_index(("gx", "gy"))
    earlier = onehot(iota((256, 256), 0) < iota((256, 256), 1))
    repeat = onehot(iota((32, 256), 0) == (iota((32, 256), 1) & 31))
    of_line = iota((8, 256), 0) == (iota((8, 256), 1) >> 5)
    carry = jnp.zeros((128, 1), F32)
    for x in range(8):
        repeated = dot(owner[x].astype(F32).astype(BF16), repeat)
        device = jnp.sum(jnp.where(of_line, repeated, 0.0), axis=0, keepdims=True).astype(I32)
        hits = onehot(iota((128, 256), 0) == device)
        before = dot(hits, earlier) + carry
        hits = hits.astype(F32)
        rank = jnp.sum(hits * before, axis=0, keepdims=True).astype(I32)
        carry = carry + jnp.sum(hits, axis=1, keepdims=True)
        rank = jnp.minimum(rank, 15)
        slot = (rank >> 3) * 1024 + device * 8 + (rank & 7)
        slots[x] = jnp.where(device == here, -1, slot)


def coarse_kernel(
    w, restricted, kappa, members, members_t, first_half, second_half, rest_faces, senders, back, xa, xb, ya, yb, fix_out, oxa, oxb, oya, oyb, coarse
):
    left, right, down, up = side_changes(rest_faces, (xa, xb, ya, yb), 8)
    mask = line_mask(8)
    for x in range(8):
        here = slice(x * 128, (x + 1) * 128)
        first, middle, final = down[:, here], jnp.zeros((8, 768), F32), up[:, here]
        if x in (0, 7):
            edge = left if x == 0 else right
            first, middle, final = first + edge[:, :128], edge[:, 128:-128], final + edge[:, -128:]
        fine = restricted[x] - jnp.concatenate([first, middle, final], axis=1)
        high = fine.astype(BF16).astype(F32)
        low = fine - high
        for half in range(2):
            group = 2 * x + half
            lanes = [slice(128 * y, 128 * y + 128) for y in range(4 * half, 4 * half + 4)]
            stack = jnp.concatenate([part[:, lane] for lane in lanes for part in (high, low)], axis=0)
            sums = dot(stack.astype(BF16), members_t[group])
            known = sum(
                jnp.where(mask[i], sums[16 * i : 16 * i + 8] + sums[16 * i + 8 : 16 * i + 16], 0.0) for i in range(4)
            )
            coarse[:, 128 * group : 128 * group + 128] = known
    fix = jnp.concatenate(
        [
            jnp.concatenate(
                [
                    jnp.sum(blocks[8 * p : 8 * p + 8, :] * coarse[:, lanes], axis=0, keepdims=True)
                    for blocks, lanes in ((first_half, slice(0, 1024)), (second_half, slice(1024, 2048)))
                ],
                axis=1,
            )
            for p in range(8)
        ],
        axis=0,
    )
    fix_out[...] = fix
    high = fix.astype(BF16).astype(F32)
    low = fix - high

    def spread_lines(x, wanted):
        out = {}
        for half in range(2):
            group = 2 * x + half
            lanes = slice(128 * group, 128 * group + 128)
            lines = [i for i in range(4) if 4 * half + i in wanted]
            stack = jnp.concatenate(
                [jnp.where(mask[i], part[:, lanes], 0.0) for i in lines for part in (high, low)], axis=0
            )
            spread = dot(stack.astype(BF16), members[group]).astype(BF16)
            for n, i in enumerate(lines):
                out[4 * half + i] = spread[16 * n : 16 * n + 16]
        return out

    def corrected(lines):
        spread = jnp.concatenate([spreads[x][y] for x, y in lines], axis=1)
        weight = jnp.concatenate([kappa[x, y : y + 1, :] for x, y in lines], axis=1)
        old = jnp.concatenate([w[x, :, 128 * y : 128 * y + 128] for x, y in lines], axis=1)
        return (old + dot(back[...], spread) * weight).astype(BF16)

    spreads = [spread_lines(x, range(8) if x in (0, 7) else (0, 7)) for x in range(8)]
    rows = {x: corrected([(x, y) for y in range(8)]) for x in (0, 7)}
    ends = {y: corrected([(x, y) for x in range(1, 7)]) for y in (0, 7)}

    def end(x, lanes):
        if x in rows:
            return rows[x][:, lanes]
        return ends[lanes.start // 128][:, 128 * (x - 1) : 128 * x]

    send_faces(senders[0], senders[1], lambda x: rows[x], end, (oxa, oxb, oya, oyb))


def corrected_inner_kernel(w, fix, kappa, members, back, c, matrix, w_new, wb_new, wb, spreads):
    mask = line_mask(8)
    high = fix[...].astype(BF16).astype(F32)
    low = fix[...] - high

    for x in range(8):
        for half in range(2):
            group = 2 * x + half
            lanes = slice(128 * group, 128 * group + 128)
            stack = jnp.concatenate(
                [jnp.where(mask[i], part[:, lanes], 0.0) for i in range(4) for part in (high, low)], axis=0
            )
            spread = dot(stack.astype(BF16), members[group]).astype(BF16)
            for i in range(4):
                y = 4 * half + i
                spreads[x, :, 128 * y : 128 * y + 128] = spread[16 * i : 16 * i + 16]
    for x in range(8):
        weight = jnp.concatenate([kappa[x, y : y + 1, :] for y in range(8)], axis=1)
        new = w[x] + dot(back[...], spreads[x]) * weight
        w_new[x] = new
        wb[x] = new.astype(BF16)
    for x in range(8):
        new = w_new[x] + c[x] - change_of(matrix, wb, x, 64)
        w_new[x] = new
        wb_new[x] = new.astype(BF16)


def from_lines(x, line, store):
    for k in range(4):
        for half in range(2):
            rows = slice(16 * k + 8 * half, 16 * k + 8 * half + 8)
            tiles = jnp.swapaxes(jnp.stack([line(y)[rows] for y in range(8)], axis=0), 0, 1)
            for m in range(8):
                store(4 * (8 * half + m) + k, tiles[m])


def last_inner_kernel(w, wb, c, matrix, kappa, out):
    for x in range(8):
        new = w[x] + c[x] - change_of(matrix, wb, x, 64)
        scale = 1.0 / kappa[x]

        def store(q, tile):
            out[q, x] = tile * scale

        from_lines(x, lambda y: new[:, 128 * y : 128 * y + 128], store)


def last_sides_kernel(old, faces, kappa, xa, xb, ya, yb, out, new, sem):
    left, right, down, up = side_changes(faces, (xa, xb, ya, yb), 64)
    zero = jnp.zeros((64, 128), F32)
    copies = []
    for x in range(8):
        here = slice(x * 128, (x + 1) * 128)
        lines = [down[:, here]] + [zero] * 6 + [up[:, here]]
        if x in (0, 7):
            edge = left if x == 0 else right
            lines = [lines[y] + edge[:, 128 * y : 128 * y + 128] for y in range(8)]
        scale = 1.0 / kappa[x]

        def store(q, tile):
            new[q, x] = old[q, x] - tile * scale

        from_lines(x, lambda y: lines[y], store)
        copies.append(pltpu.make_async_copy(new.at[:, x], out.at[:, x], sem.at[x]))
        copies[-1].start()
    for copy in copies:
        copy.wait()


def pack_kernel(inverse_hbm, places_hbm, out, stage, inverse, places, sem):
    copies = [pltpu.make_async_copy(inverse_hbm, inverse, sem.at[0]), pltpu.make_async_copy(places_hbm, places, sem.at[1])]
    for copy in copies:
        copy.start()
    for copy in copies:
        copy.wait()
    table = jnp.concatenate([inverse[:, 128 * n : 128 * n + 128].astype(BF16) for n in range(16)], axis=0)
    numbers = iota((128, 256), 0)
    rows = []
    for r in range(8):
        wanted = jnp.concatenate([places[r : r + 1, :], places[r + 8 : r + 9, :]], axis=1)
        parts = dot(table, onehot(numbers == (wanted & 127)))
        part = wanted >> 7
        chosen = sum(jnp.where(part == n, parts[64 * n : 64 * n + 64], 0.0) for n in range(16))
        rows.append(jnp.concatenate([chosen[:, :128], chosen[:, 128:]], axis=0))
    for r in range(8):
        stage[pl.ds(r, 128, stride=8), :] = jnp.transpose(rows[r])
    out[...] = stage[...].reshape(128, 8, 128).astype(BF16)


def unpack_kernel(start, arrived, inverse, slots, total, out):
    turned = jnp.transpose(arrived[...].astype(F32).reshape(1024, 128))
    table = jnp.concatenate([turned[:64], turned[64:]], axis=1).astype(BF16)
    numbers = iota((2048, 256), 0)
    for n in range(4):
        x = start + n
        slot = slots[x]
        far = dot(table, onehot(numbers == slot))
        weight = jnp.concatenate([total[2 * x], total[2 * x + 1]], axis=1)
        own = inverse[:, 256 * x : 256 * x + 256]
        out[:, 256 * n : 256 * n + 256] = jnp.where(slot < 0, own, far) / weight


VMEM_SPEC = pl.BlockSpec(memory_space=pltpu.VMEM)
HBM_SPEC = pl.BlockSpec(memory_space=pl.ANY)


def run(body, ins, outs, scratch=(), in_hbm=(), out_hbm=(), anywhere=(), aliases=None):
    ins = [pltpu.with_memory_space_constraint(x, pltpu.HBM) if i in in_hbm else x for i, x in enumerate(ins)]
    outs = [pltpu.HBM(x.shape, x.dtype) if i in out_hbm else x for i, x in enumerate(outs)]
    return pl.pallas_call(
        body,
        out_shape=outs,
        in_specs=[HBM_SPEC if i in in_hbm or i in anywhere else VMEM_SPEC for i in range(len(ins))],
        out_specs=[HBM_SPEC if i in out_hbm else VMEM_SPEC for i in range(len(outs))],
        scratch_shapes=list(scratch),
        input_output_aliases=aliases or {},
        compiler_params=pltpu.CompilerParams(vmem_limit_bytes=LIMIT),
    )(*ins)


def array(shape, dtype):
    return jax.ShapeDtypeStruct(shape, dtype)


def per_device(
    u_init, rhs, kappa, block_diagonal, face_coupling, smoother, restriction, coarse_inverse, segment_id, owner_device, arrival_place
):
    faces_shape = [array((16, 1024), BF16)] * 4
    state = [array((8, 64, 1024), F32), array((8, 64, 1024), BF16)]
    inverse = coarse_inverse.reshape(64, 2048)
    places = jnp.transpose(arrival_place[0])
    coupling_t = jnp.transpose(face_coupling, (0, 2, 1))

    (packed,) = run(
        pack_kernel,
        (inverse, places),
        [array((128, 8, 128), BF16)],
        [
            pltpu.VMEM((1024, 128), F32),
            pltpu.VMEM((64, 2048), F32),
            pltpu.VMEM((16, 128), I32),
            pltpu.SemaphoreType.DMA((2,)),
        ],
        in_hbm=(0, 1),
    )
    arrived = lax.all_to_all(packed, ("gx", "gy"), split_axis=0, concat_axis=0, tiled=True)
    natural_scratch = pltpu.VMEM((64, 8, 8, 128), BF16)
    lines_scratch = pltpu.VMEM((8, 64, 1024), BF16)
    sends = run(
        start_kernel,
        (u_init, kappa, packed),
        faces_shape,
        [natural_scratch, pltpu.VMEM((8, 8, 128), F32), lines_scratch]
        + [pltpu.VMEM((16, 1024), BF16)] * 4
        + [pltpu.SemaphoreType.DMA((5,)), pltpu.SemaphoreType.DMA((4,))],
        in_hbm=(0, 1, 2),
        out_hbm=range(4),
    )
    received = exchange(sends)
    matrix, rest, faces, rest_faces, senders, back, w, wb, c, cr = run(
        first_inner_kernel,
        (u_init, rhs, kappa, arrived, block_diagonal, coupling_t, smoother, restriction),
        [
            array((128, 256), BF16),
            array((16, 256), BF16),
            array((2, 256, 32), BF16),
            array((2, 32, 32), BF16),
            array((2, 32, 128), BF16),
            array((64, 16), BF16),
        ]
        + state
        + [array((8, 64, 1024), F32), array((8, 8, 1024), F32)],
        [pltpu.VMEM((80, 64), BF16)]
        + [natural_scratch] * 2
        + [lines_scratch] * 2
        + [pltpu.VMEM((8, 8, 128), F32), pltpu.SemaphoreType.DMA((2, 4)), pltpu.SemaphoreType.DMA],
        in_hbm=(0, 1, 2),
        anywhere=(3,),
    )
    members, members_t, total, slots = run(
        members_kernel,
        (segment_id, kappa, owner_device),
        [array((16, 128, 128), BF16)] * 2 + [array((16, 1, 128), F32), array((8, 1, 256), I32)],
    )
    halves = [
        run(functools.partial(unpack_kernel, start), (arrived, inverse, slots, total), [array((64, 1024), F32)])[0]
        for start in (0, 4)
    ]

    def sides(w, wb, received, after):
        w, wb, *sends = run(
            sides_kernel,
            (w, wb, faces, senders, after, *received),
            state + faces_shape,
            anywhere=(4,),
            aliases={0: 0, 1: 1},
        )
        return w, wb, exchange(sends)

    w, wb, *sends = run(
        first_sides_kernel,
        (w, wb, faces, senders, *received),
        state + faces_shape,
        [pltpu.VMEM((16, 1024), BF16)] * 4 + [pltpu.SemaphoreType.DMA((4,))],
        anywhere=(4, 5, 6, 7),
        aliases={0: 0, 1: 1},
    )
    received = exchange(sends)
    for after in (members, halves[0]):
        w, wb = run(inner_kernel, (w, wb, c, matrix), state)
        w, wb, received = sides(w, wb, received, after)
    (restricted,) = run(rest_kernel, (wb, cr, rest), [array((8, 8, 1024), F32)])
    fix, *sends = run(
        coarse_kernel,
        (w, restricted, kappa, members, members_t, *halves, rest_faces, senders, back, *received),
        [array((8, 2048), F32)] + faces_shape,
        [pltpu.VMEM((8, 2048), F32)],
    )
    received = exchange(sends)
    w, wb = run(corrected_inner_kernel, (w, fix, kappa, members, back, c, matrix), state, [lines_scratch, pltpu.VMEM((8, 16, 1024), BF16)])
    w, wb, received = sides(w, wb, received, members)
    w, wb = run(inner_kernel, (w, wb, c, matrix), state)
    w, wb, received = sides(w, wb, received, members)
    (out,) = run(last_inner_kernel, (w, wb, c, matrix, kappa), [array((64, 8, 8, 128), F32)])
    (out,) = run(
        last_sides_kernel,
        (out, faces, kappa, *received),
        [array((64, 8, 8, 128), F32)],
        [pltpu.VMEM((64, 8, 8, 128), F32), pltpu.SemaphoreType.DMA((8,))],
        out_hbm=(0,),
    )
    return out


def solution(mesh):
    return jax.shard_map(
        per_device,
        mesh=mesh,
        in_specs=(
            P(None, "gx", "gy", None),
            P(None, "gx", "gy", None),
            P("gx", "gy", None),
            P(),
            P(),
            P(),
            P(),
            P(None, None, ("gx", "gy")),
            P("gx", "gy", None),
            P("gx", "gy", None),
            P(("gx", "gy"), None, None),
        ),
        out_specs=P(None, "gx", "gy", None),
        check_vma=False,
    )
```
